32 devices in a mesh: head: 4 (over x, core), blk: 8 (over z, y).
Axes of the slice: x: 2, y: 2, z: 4, core: 2. Of those that a mesh axis runs over, the one named last changes fastest.
Arguments:
- queries: bfloat16 [1, 2816, 640], P(None, ('blk', 'head')), may hold values from -6 to 6
- keys: bfloat16 [1, 2816, 640], P(None, ('blk', 'head')), may hold values from -6 to 6
- values: bfloat16 [1, 2816, 640], P(None, ('blk', 'head')), may hold values from -6 to 6
- outputs: bfloat16 [1, 2816, 640], P(None, ('blk', 'head')), may hold values from -6 to 6
- grad_out: bfloat16 [1, 2816, 640], P(None, ('blk', 'head')), may hold values from -384 to 384
- lse: float32 [1, 8, 2816], P(None, 'head', 'blk'), may hold values from 8.5 to 10
Outputs:
- grad_queries: bfloat16 [1, 2816, 640], P(None, ('blk', 'head'))
- grad_keys: bfloat16 [1, 2816, 640], P(None, ('blk', 'head'))
- grad_values: bfloat16 [1, 2816, 640], P(None, ('blk', 'head'))
The draws below stay inside these ranges and needn't reach their ends.
All inputs are finite; a program needn't handle non-finite values.
Results may differ from the reference program's by a relative error of at most 0.0085.
Values may be sent and summed in bfloat16 or wider, within the bound.
No kernel may reach another device: no remote copies, remote signals or barrier semaphores. Data moves between devices by JAX's collectives and lax.ppermute only.
A program may use at most 64 MiB of HBM per device.

```python
import jax
import jax.numpy as jnp
from jax import lax

HEADS = 8
HDIM = 80
SEQS = 1
SEQ_DEV = 88
D = 640
TOKENS = 2816
N_HEAD = 4


def block_levels(stream_key, extent, split, smallest, top_value):
    level = 1.0
    for axis_at, blocks in split:
        steps = jax.random.uniform(jax.random.fold_in(jax.random.fold_in(stream_key, 6), axis_at), (blocks,), jnp.float32, smallest / len(split), top_value / len(split))
        level = level * jnp.repeat(jnp.exp(steps), extent[axis_at] // blocks).reshape((-1,) + (1,) * (len(extent) - 1 - axis_at))
    return level


def noise(stream_key, extent, scale, limit, cuts=(), dtype=jnp.bfloat16):
    factor_of = block_levels(stream_key, extent, cuts, -0.22, 0.18) if cuts else 1.0
    drawn = jax.random.normal(stream_key, extent, jnp.float32) * scale * factor_of
    return jnp.minimum(jnp.maximum(drawn, -limit), limit).astype(dtype)


def setup_inputs(seed: int = 0) -> dict:
    arg_keys = jax.random.split(jax.random.key(seed), 7)
    queries = noise(arg_keys[0], (SEQS, TOKENS, D), 1.0, 6.0, ((1, 32),))
    keys = noise(arg_keys[1], (SEQS, TOKENS, D), 1.0, 6.0, ((1, 32),))
    values = noise(arg_keys[2], (SEQS, TOKENS, D), 1.0, 6.0, ((1, 32),))
    outputs = noise(arg_keys[3], (SEQS, TOKENS, D), 1.0, 6.0, ((1, 32),))
    grad_out = noise(arg_keys[4], (SEQS, TOKENS, D), 64.0, 384.0, ((1, 32),))
    lse = jnp.clip(8.5 + 1.5 * jax.random.uniform(arg_keys[5], (SEQS, HEADS, TOKENS), jnp.float32) ** block_levels(arg_keys[5], (SEQS, HEADS, TOKENS), ((1, 4), (2, 8)), -0.2, 0.2), 8.5, 10.0)
    return dict(queries=queries, keys=keys, values=values, outputs=outputs, grad_out=grad_out, lse=lse)


def head_grads(query_h, key_h, value_h, output_h, cotan_h, lse_h):
    scaling = HDIM ** -0.5
    block_rows = SEQ_DEV * N_HEAD
    nblocks = TOKENS // block_rows
    delta_h = jnp.sum(cotan_h.astype(jnp.float32) * output_h.astype(jnp.float32), axis=-1)
    query_blocks = query_h.reshape(nblocks, block_rows, HDIM)
    cotan_blocks = cotan_h.reshape(nblocks, block_rows, HDIM)
    lse_blocks = lse_h.reshape(nblocks, block_rows)
    delta_blocks = delta_h.reshape(nblocks, block_rows)

    def one_block(carry, pieces):
        acc_keys, acc_values = carry
        query_b, cotan_b, lse_b, delta_b = pieces
        scores = jnp.dot(query_b, key_h.T, preferred_element_type=jnp.float32) * scaling
        probs = jnp.exp(scores - lse_b[:, None])
        probs16 = probs.astype(jnp.bfloat16)
        acc_values = acc_values + jnp.dot(probs16.T, cotan_b, preferred_element_type=jnp.float32)
        dprobs = jnp.dot(cotan_b, value_h.T, preferred_element_type=jnp.float32)
        dscores = (probs * (dprobs - delta_b[:, None])).astype(jnp.bfloat16)
        grad_q = jnp.dot(dscores, key_h, preferred_element_type=jnp.float32) * scaling
        acc_keys = acc_keys + jnp.dot(dscores.T, query_b, preferred_element_type=jnp.float32)
        return (acc_keys, acc_values), grad_q.astype(jnp.bfloat16)

    start = (jnp.zeros((TOKENS, HDIM), jnp.float32), jnp.zeros((TOKENS, HDIM), jnp.float32))
    (acc_keys, acc_values), grad_q = lax.scan(one_block, start, (query_blocks, cotan_blocks, lse_blocks, delta_blocks))
    return (grad_q.reshape(TOKENS, HDIM), (acc_keys * scaling).astype(jnp.bfloat16), acc_values.astype(jnp.bfloat16))


def by_heads(array):
    return jnp.transpose(array.reshape(TOKENS, HEADS, HDIM), (1, 0, 2))


def back_to_rows(array):
    return jnp.transpose(array, (1, 0, 2)).reshape(TOKENS, HEADS * HDIM)


def one_crop(pieces):
    queries, keys, values, outputs, grad_out, lse = pieces
    stacked = (by_heads(queries), by_heads(keys), by_heads(values), by_heads(outputs), by_heads(grad_out), lse)
    grad_q, grad_k, grad_v = lax.map(lambda parts: head_grads(*parts), stacked)
    return back_to_rows(grad_q), back_to_rows(grad_k), back_to_rows(grad_v)


def reference(queries, keys, values, outputs, grad_out, lse):
    grad_q, grad_k, grad_v = lax.map(one_crop, (queries, keys, values, outputs, grad_out, lse))
    return grad_q, grad_k, grad_v
```

```python
import functools
import math

import jax
import jax.numpy as jnp
from jax import lax
from jax.experimental import pallas as pl
from jax.experimental.pallas import tpu as pltpu
from jax.sharding import PartitionSpec as P

HDIM = 80
SCALING = HDIM ** (-0.5)
LOG2E = math.log2(math.e)
PADDED = 96
VMEM_LIMIT = 24 * 1024 * 1024
F32 = jnp.float32
BF16 = jnp.bfloat16


def shifted(block, axis, distance):
    devices = range(lax.axis_size(axis))
    route = [((i - distance) % len(devices), i) for i in devices]
    return lax.ppermute(block, axis, route)


def tile_terms(query_h, cotan_h, lse_rows, delta_rows, key_h, value_h):
    query_rows = query_h.shape[0]
    key_rows = key_h.shape[0]
    groups = query_h.shape[1]
    scores = (
        jnp.einsum("qhd,khd->hqk", query_h, key_h, preferred_element_type=jnp.float32) * SCALING
    )
    probs = jnp.exp(scores - lse_rows[:, :, None])
    probs16 = probs.astype(jnp.bfloat16)
    value_part = jnp.einsum("hqk,qhd->khd", probs16, cotan_h, preferred_element_type=jnp.float32)
    dprobs = jnp.einsum("qhd,khd->hqk", cotan_h, value_h, preferred_element_type=jnp.float32)
    dscores = (probs * (dprobs - delta_rows[:, :, None])).astype(jnp.bfloat16)
    query_part = jnp.einsum("hqk,khd->qhd", dscores, key_h, preferred_element_type=jnp.float32)
    key_part = jnp.einsum("hqk,qhd->khd", dscores, query_h, preferred_element_type=jnp.float32)
    return (
        query_part.reshape(query_rows, groups * HDIM),
        key_part.reshape(key_rows, groups * HDIM),
        value_part.reshape(key_rows, groups * HDIM),
    )


def crop_terms(query_h, cotan_h, lse_rows, delta_rows, key_h, value_h):
    return lax.map(
        lambda pieces: tile_terms(*pieces), (query_h, cotan_h, lse_rows, delta_rows, key_h, value_h)
    )


def ring_body(queries, keys, values, outputs, grad_out, lse):
    crops = queries.shape[0]
    groups = lse.shape[1]
    rows = lse.shape[2]
    query_own, key_own, value_own, cotan_own, output_own = (
        lax.all_to_all(sent, "head", split_axis=2, concat_axis=1, tiled=True)
        for sent in (queries, keys, values, grad_out, outputs)
    )
    products = cotan_own.astype(jnp.float32) * output_own.astype(jnp.float32)
    delta_rows = jnp.transpose(
        jnp.sum(products.reshape(crops, rows, groups, HDIM), axis=-1), (0, 2, 1)
    )
    query_h = query_own.reshape(crops, rows, groups, HDIM)
    cotan_h = cotan_own.reshape(crops, rows, groups, HDIM)
    key_h = key_own.reshape(crops, rows, groups, HDIM)
    value_h = value_own.reshape(crops, rows, groups, HDIM)
    width = groups * HDIM
    nblocks = lax.axis_size("blk")
    zeros_acc = jnp.zeros((crops, rows, width), jnp.float32)
    start = (query_h, cotan_h, lse, delta_rows, zeros_acc, zeros_acc, zeros_acc)

    def cycle_step(index, carry):
        query_cur, cotan_cur, lse_cur, delta_cur, query_acc, key_acc, value_acc = carry
        query_part, key_part, value_part = crop_terms(
            query_cur, cotan_cur, lse_cur, delta_cur, key_h, value_h
        )
        query_acc, lse_cur, delta_cur = shifted(
            (query_acc + query_part, lse_cur, delta_cur), "blk", 1
        )
        query_cur, cotan_cur = shifted((query_cur, cotan_cur), "blk", 1)
        return (
            query_cur,
            cotan_cur,
            lse_cur,
            delta_cur,
            query_acc,
            key_acc + key_part,
            value_acc + value_part,
        )

    query_cur, cotan_cur, lse_cur, delta_cur, query_acc, key_acc, value_acc = lax.fori_loop(
        0, nblocks - 1, cycle_step, start
    )
    query_part, key_part, value_part = crop_terms(
        query_cur, cotan_cur, lse_cur, delta_cur, key_h, value_h
    )
    query_total = shifted((query_acc + query_part).astype(jnp.bfloat16), "blk", 1).astype(
        jnp.float32
    )
    grad_q16 = (query_total * SCALING).astype(jnp.bfloat16)
    grad_k16 = ((key_acc + key_part) * SCALING).astype(jnp.bfloat16)
    grad_v16 = (value_acc + value_part).astype(jnp.bfloat16)
    return tuple(
        lax.all_to_all(grad, "head", split_axis=1, concat_axis=2, tiled=True)
        for grad in (grad_q16, grad_k16, grad_v16)
    )


def call(kernel, out_shape, *operands, scratch=()):
    specs = [
        pl.BlockSpec(memory_space=pltpu.SMEM if a.dtype == jnp.int32 else pltpu.VMEM)
        for a in operands
    ]
    return pl.pallas_call(
        kernel,
        out_shape=out_shape,
        in_specs=specs,
        out_specs=jax.tree.map(lambda _: pl.BlockSpec(memory_space=pltpu.VMEM), out_shape),
        scratch_shapes=list(scratch),
        compiler_params=pltpu.CompilerParams(vmem_limit_bytes=VMEM_LIMIT),
    )(*operands)


def shape(*dims, dtype=BF16):
    return jax.ShapeDtypeStruct(dims, dtype)


def head_of(array, head):
    return array[:, HDIM * head : HDIM * (head + 1)]


def pieces_of(column):
    high = column.astype(BF16)
    rest = column - high.astype(F32)
    middle = rest.astype(BF16)
    low = (rest - middle.astype(F32)).astype(BF16)
    return [high.astype(F32), middle.astype(F32), low.astype(F32)]


def pack_queries_kernel(place, q_ref, do_ref, o_ref, out_ref):
    x, w, c = place[0], place[1], place[2]
    rows = q_ref.shape[0]
    q = q_ref[...].astype(F32)
    do = do_ref[...].astype(F32)
    products = do * o_ref[...].astype(F32)
    zeros = jnp.zeros((rows, 58), F32)
    for xs in range(2):
        for ws in range(2):
            sides, deltas = [], []
            for cs in range(2):
                head = 4 * xs + 2 * cs + ws
                sides.append(jnp.concatenate([head_of(q, head), head_of(do, head)], axis=1))
                delta = jnp.sum(head_of(products, head), axis=1, keepdims=True)
                deltas.append(jnp.concatenate(pieces_of(delta), axis=1))
            kept = jnp.where(c == 0, sides[0], sides[1])
            given = jnp.where(c == 0, sides[1], sides[0])
            kept_delta = jnp.where(c == 0, deltas[0], deltas[1])
            given_delta = jnp.where(c == 0, deltas[1], deltas[0])
            row = jnp.concatenate([kept, given, kept_delta, given_delta, zeros], axis=1)
            out_ref[2 * (x ^ xs) + (w ^ ws)] = row.astype(BF16)


def pack_keys_kernel(place, k_ref, v_ref, out_ref):
    x, w, c = place[0], place[1], place[2]
    rows = k_ref.shape[0]
    k = k_ref[...].astype(F32)
    v = v_ref[...].astype(F32)
    zeros = jnp.zeros((rows, 64), F32)
    for xs in range(2):
        for ws in range(2):
            sides = []
            for cs in range(2):
                head = 4 * xs + 2 * cs + ws
                sides.append(jnp.concatenate([head_of(k, head), head_of(v, head)], axis=1))
            kept = jnp.where(c == 0, sides[0], sides[1])
            given = jnp.where(c == 0, sides[1], sides[0])
            row = jnp.concatenate([kept, given, zeros], axis=1)
            out_ref[2 * (x ^ xs) + (w ^ ws)] = row.astype(BF16)


def lined_up(own, near, other):
    blocks = []
    for j in range(4):
        held = own if j == 0 else near[j - 1][...]
        blocks.append(held[:, :160].astype(F32))
        blocks.append(other[j][:, 32:192].astype(F32))
    return jnp.concatenate(blocks, axis=1).astype(BF16)


def gather_queries_kernel(place, own, near1, near2, near3, other, lse_own, lse_near, wide, aux, tall):
    rows = wide.shape[0]
    near = (near1, near2, near3)
    wide[...] = lined_up(own[0], near, other)
    pad = jnp.zeros((PADDED - rows, 128), BF16)
    for j in range(4):
        held = own[0] if j == 0 else near[j - 1][...]
        tall[2 * j, 0:rows] = held[:, 256:384]
        tall[2 * j + 1, 0:rows] = other[j][:, 128:256]
        tall[2 * j, rows:PADDED] = pad
        tall[2 * j + 1, rows:PADDED] = pad
    spots = tall[...].reshape(8 * PADDED, 128)
    row = lax.broadcasted_iota(jnp.int32, (8, 128), 0)
    lane = lax.broadcasted_iota(jnp.int32, (8, 128), 1)
    first = 64 + 3 * row
    chosen = jnp.where((row < 2) & (lane >= first) & (lane < first + 3), 1.0, 0.0).astype(BF16)
    sums = lax.dot_general(
        chosen, spots, (((1,), (1,)), ((), ())), preferred_element_type=F32
    )
    at = lax.broadcasted_iota(jnp.int32, (1, 8 * PADDED), 1)
    odd = lax.rem(lax.div(at, PADDED), 2)
    delta = jnp.where(odd == 0, sums[0:1], sums[1:2])
    h = place[3]
    parts = []
    for i in range(8):
        source = lse_near if (i // 2) % 2 else lse_own
        part = source[pl.ds(h ^ (2 * (i // 4) + i % 2), 1), :]
        parts += [part, jnp.zeros((1, PADDED - rows), F32)]
    lse = jnp.concatenate(parts, axis=1) * LOG2E
    aux[...] = jnp.concatenate([lse, delta], axis=0)


def gather_keys_kernel(own, near1, near2, near3, other, wide):
    wide[...] = lined_up(own[0], (near1, near2, near3), other)


def spread(wide_ref, left, right):
    rows = wide_ref.shape[0]
    wide = wide_ref[...].astype(F32)
    pad = jnp.zeros((PADDED - rows, HDIM), F32)
    for i in range(8):
        at = 2 * HDIM * i
        spot = pl.ds(PADDED * i, PADDED)
        left[spot, :] = jnp.concatenate([wide[:, at : at + HDIM], pad], axis=0).astype(BF16)
        right[spot, :] = jnp.concatenate(
            [wide[:, at + HDIM : at + 2 * HDIM], pad], axis=0
        ).astype(BF16)


def tile_step(q_wide, aux, k_wide, scratch, chunk):
    q_s, do_s, k_s, v_s = scratch
    spread(q_wide, q_s, do_s)
    spread(k_wide, k_s, v_s)
    q, do = q_s[...], do_s[...]
    q_t, do_t = q.T, do.T
    k_t = k_s[...].T
    lse, delta = aux[0:1, :], aux[1:2, :]
    total = q.shape[0]
    dq_t = None
    parts = []
    for start in range(0, total, chunk):
        spot = slice(start, start + chunk)
        k, v = k_s[spot, :], v_s[spot, :]
        scores = jnp.dot(k, q_t, preferred_element_type=F32)
        probs = jnp.exp2(scores * (SCALING * LOG2E) - lse)
        dv = jnp.dot(probs.astype(BF16), do, preferred_element_type=F32)
        dprobs = jnp.dot(v, do_t, preferred_element_type=F32)
        dscores = (probs * (dprobs - delta)).astype(BF16)
        dk = jnp.dot(dscores, q, preferred_element_type=F32)
        more = jnp.dot(k_t[:, spot], dscores, preferred_element_type=F32)
        dq_t = more if dq_t is None else dq_t + more
        parts.append((spot, dk, dv))
    return dq_t, parts


CHUNK = 256


def own_own_kernel(q_wide, aux, k_wide, dq_t, dk, dv, *scratch):
    dq_t[...], parts = tile_step(q_wide, aux, k_wide, scratch, CHUNK)
    for spot, dk_part, dv_part in parts:
        dk[spot, :] = dk_part
        dv[spot, :] = dv_part


def own_far_kernel(q_wide, aux, k_wide, dq_before, dq_t, dk, dv, *scratch):
    more, parts = tile_step(q_wide, aux, k_wide, scratch, CHUNK)
    dq_t[...] = dq_before[...] + more
    for spot, dk_part, dv_part in parts:
        dk[spot, :] = dk_part
        dv[spot, :] = dv_part


def far_far_kernel(q_wide, aux, k_wide, dk_before, dv_before, dq_t, wire, dk, dv, *scratch):
    dq_t[...], parts = tile_step(q_wide, aux, k_wide, scratch, CHUNK)
    for spot, dk_part, dv_part in parts:
        dk[spot, :] = (dk_before[spot, :] + dk_part) * SCALING
        dv[spot, :] = dv_before[spot, :] + dv_part
    rows = wire.shape[0]
    blocks = []
    for i in range(8):
        spot = slice(PADDED * i, PADDED * i + rows)
        blocks += [dk[spot, :], dv[spot, :]]
    wire[...] = jnp.concatenate(blocks, axis=1).astype(BF16)


def far_own_kernel(q_wide, aux, k_wide, dq_before, dk_before, dv_before, wire, dk, dv, *scratch):
    more, parts = tile_step(q_wide, aux, k_wide, scratch, CHUNK)
    dq = ((dq_before[...] + more) * SCALING).T
    rows = wire.shape[0]
    wire[...] = jnp.concatenate(
        [dq[PADDED * i : PADDED * i + rows] for i in range(8)], axis=1
    ).astype(BF16)
    for spot, dk_part, dv_part in parts:
        dk[spot, :] = dk_before[spot, :] + dk_part
        dv[spot, :] = dv_before[spot, :] + dv_part


def pack_grads_kernel(dq_t, dk, dv, dq_wire, dkv_wire, out):
    rows = dq_wire.shape[0]
    dq = dq_t[...].T
    dq_far = dq_wire[...].astype(F32)
    dkv_far = dkv_wire[...].astype(F32)
    zeros = jnp.zeros((rows, 16), F32)
    for i in range(8):
        spot = slice(PADDED * i, PADDED * i + rows)
        at = 2 * HDIM * i
        block = jnp.concatenate(
            [
                dq[spot] * SCALING + dq_far[:, HDIM * i : HDIM * (i + 1)],
                dk[spot, :] * SCALING + dkv_far[:, at : at + HDIM],
                dv[spot, :] + dkv_far[:, at + HDIM : at + 2 * HDIM],
                zeros,
            ],
            axis=1,
        )
        out[i // 2, :, 256 * (i % 2) : 256 * (i % 2) + 256] = block.astype(BF16)


def unpack_grads_kernel(place, held, other, dq, dk, dv):
    x, w, c = place[0], place[1], place[2]
    blocks = []
    for head in range(8):
        xs, cs, ws = head // 4, (head // 2) % 2, head % 2
        j = 2 * (x ^ xs) + (w ^ ws)
        blocks.append(
            jnp.where(c == cs, held[j][:, :256].astype(F32), other[j].astype(F32))
        )
    for k, out in enumerate((dq, dk, dv)):
        out[...] = jnp.concatenate(
            [block[:, HDIM * k : HDIM * (k + 1)] for block in blocks], axis=1
        ).astype(BF16)


def flipped(array, head_bits, blk_bits):
    heads, blks = lax.axis_size("head"), lax.axis_size("blk")
    if not blk_bits:
        return lax.ppermute(array, "head", [(i, i ^ head_bits) for i in range(heads)])
    if not head_bits:
        return lax.ppermute(array, "blk", [(i, i ^ blk_bits) for i in range(blks)])
    bits = head_bits * blks + blk_bits
    return lax.ppermute(array, ("head", "blk"), [(i, i ^ bits) for i in range(heads * blks)])


def to_chips(packed):
    return [flipped(packed[1], 0, 2), flipped(packed[2], 2, 0), flipped(packed[3], 2, 2)]


def grid_body(queries, keys, values, outputs, grad_out, lse):
    rows = queries.shape[1]
    h, b = lax.axis_index("head"), lax.axis_index("blk")
    x, c, w = h // 2, h % 2, (b // 2) % 2
    place = jnp.stack([x, w, c, h]).astype(jnp.int32)
    padded = 8 * PADDED
    tile_scratch = [pltpu.VMEM((padded, HDIM), BF16)] * 4

    packed_q = call(
        pack_queries_kernel, shape(4, rows, 384), place, queries[0], grad_out[0], outputs[0]
    )
    near_q = to_chips(packed_q)
    packed_k = call(pack_keys_kernel, shape(4, rows, 384), place, keys[0], values[0])
    near_k = to_chips(packed_k)
    lse_rows = lse[0].reshape(2, 4, rows)
    lse_own = lax.dynamic_index_in_dim(lse_rows, w, 0, keepdims=False)
    lse_near = flipped(lax.dynamic_index_in_dim(lse_rows, 1 - w, 0, keepdims=False), 0, 2)

    other_q = flipped(jnp.stack([a[:, 128:] for a in [packed_q[0]] + near_q]), 1, 0)
    q_own, aux_own = call(
        gather_queries_kernel,
        (shape(rows, 1280), shape(2, padded, dtype=F32)),
        place,
        packed_q,
        *near_q,
        other_q,
        lse_own,
        lse_near,
        scratch=[pltpu.VMEM((8, PADDED, 128), BF16)],
    )
    q_far = flipped(q_own, 0, 4)
    aux_far = flipped(aux_own, 0, 4)
    other_k = flipped(jnp.stack([a[:, 128:] for a in [packed_k[0]] + near_k]), 1, 0)
    k_own = call(gather_keys_kernel, shape(rows, 1280), packed_k, *near_k, other_k)
    k_far = flipped(k_own, 0, 1)

    grad_shape = shape(padded, HDIM, dtype=F32)
    dq_shape = shape(HDIM, padded, dtype=F32)
    dq_own, dk_own, dv_own = call(
        own_own_kernel, (dq_shape, grad_shape, grad_shape), q_own, aux_own, k_own,
        scratch=tile_scratch,
    )
    dq_own, dk_far, dv_far = call(
        own_far_kernel, (dq_shape, grad_shape, grad_shape), q_own, aux_own, k_far, dq_own,
        scratch=tile_scratch,
    )
    sums = [pltpu.VMEM((padded, HDIM), F32)] * 2
    dq_far, dkv_wire = call(
        far_far_kernel, (dq_shape, shape(rows, 1280)), q_far, aux_far, k_far, dk_far, dv_far,
        scratch=sums + tile_scratch,
    )
    dkv_back = flipped(dkv_wire, 0, 1)
    dq_wire, dk_own, dv_own = call(
        far_own_kernel, (shape(rows, 640), grad_shape, grad_shape),
        q_far, aux_far, k_own, dq_far, dk_own, dv_own,
        scratch=tile_scratch,
    )
    dq_back = flipped(dq_wire, 0, 4)

    packed_g = call(
        pack_grads_kernel, shape(4, rows, 512), dq_own, dk_own, dv_own, dq_back, dkv_back
    )
    held = jnp.stack([packed_g[0]] + to_chips(packed_g))
    other = flipped(held[:, :, 256:], 1, 0)
    out = shape(rows, queries.shape[2])
    grads = call(unpack_grads_kernel, (out, out, out), place, held, other)
    return tuple(grad[None] for grad in grads)


def solution(mesh):
    placed = P(None, ("blk", "head"), None)
    on_grid = mesh.shape["head"] == 4 and mesh.shape["blk"] == 8
    return jax.shard_map(
        grid_body if on_grid else ring_body,
        mesh=mesh,
        in_specs=(placed,) * 5 + (P(None, "head", "blk"),),
        out_specs=(placed,) * 3,
        check_vma=False,
    )
```

```python
import functools
import math

import jax
import jax.numpy as jnp
from jax import lax
from jax.experimental import pallas as pl
from jax.experimental.pallas import tpu as pltpu
from jax.sharding import PartitionSpec as P

HDIM = 80
SCALING = HDIM ** (-0.5)
LOG2E = math.log2(math.e)
PADDED = 96
VMEM_LIMIT = 24 * 1024 * 1024
F32 = jnp.float32
BF16 = jnp.bfloat16


def shifted(block, axis, distance):
    devices = range(lax.axis_size(axis))
    route = [((i - distance) % len(devices), i) for i in devices]
    return lax.ppermute(block, axis, route)


def tile_terms(query_h, cotan_h, lse_rows, delta_rows, key_h, value_h):
    query_rows = query_h.shape[0]
    key_rows = key_h.shape[0]
    groups = query_h.shape[1]
    scores = (
        jnp.einsum("qhd,khd->hqk", query_h, key_h, preferred_element_type=jnp.float32) * SCALING
    )
    probs = jnp.exp(scores - lse_rows[:, :, None])
    probs16 = probs.astype(jnp.bfloat16)
    value_part = jnp.einsum("hqk,qhd->khd", probs16, cotan_h, preferred_element_type=jnp.float32)
    dprobs = jnp.einsum("qhd,khd->hqk", cotan_h, value_h, preferred_element_type=jnp.float32)
    dscores = (probs * (dprobs - delta_rows[:, :, None])).astype(jnp.bfloat16)
    query_part = jnp.einsum("hqk,khd->qhd", dscores, key_h, preferred_element_type=jnp.float32)
    key_part = jnp.einsum("hqk,qhd->khd", dscores, query_h, preferred_element_type=jnp.float32)
    return (
        query_part.reshape(query_rows, groups * HDIM),
        key_part.reshape(key_rows, groups * HDIM),
        value_part.reshape(key_rows, groups * HDIM),
    )


def crop_terms(query_h, cotan_h, lse_rows, delta_rows, key_h, value_h):
    return lax.map(
        lambda pieces: tile_terms(*pieces), (query_h, cotan_h, lse_rows, delta_rows, key_h, value_h)
    )


def ring_body(queries, keys, values, outputs, grad_out, lse):
    crops = queries.shape[0]
    groups = lse.shape[1]
    rows = lse.shape[2]
    query_own, key_own, value_own, cotan_own, output_own = (
        lax.all_to_all(sent, "head", split_axis=2, concat_axis=1, tiled=True)
        for sent in (queries, keys, values, grad_out, outputs)
    )
    products = cotan_own.astype(jnp.float32) * output_own.astype(jnp.float32)
    delta_rows = jnp.transpose(
        jnp.sum(products.reshape(crops, rows, groups, HDIM), axis=-1), (0, 2, 1)
    )
    query_h = query_own.reshape(crops, rows, groups, HDIM)
    cotan_h = cotan_own.reshape(crops, rows, groups, HDIM)
    key_h = key_own.reshape(crops, rows, groups, HDIM)
    value_h = value_own.reshape(crops, rows, groups, HDIM)
    width = groups * HDIM
    nblocks = lax.axis_size("blk")
    zeros_acc = jnp.zeros((crops, rows, width), jnp.float32)
    start = (query_h, cotan_h, lse, delta_rows, zeros_acc, zeros_acc, zeros_acc)

    def cycle_step(index, carry):
        query_cur, cotan_cur, lse_cur, delta_cur, query_acc, key_acc, value_acc = carry
        query_part, key_part, value_part = crop_terms(
            query_cur, cotan_cur, lse_cur, delta_cur, key_h, value_h
        )
        query_acc, lse_cur, delta_cur = shifted(
            (query_acc + query_part, lse_cur, delta_cur), "blk", 1
        )
        query_cur, cotan_cur = shifted((query_cur, cotan_cur), "blk", 1)
        return (
            query_cur,
            cotan_cur,
            lse_cur,
            delta_cur,
            query_acc,
            key_acc + key_part,
            value_acc + value_part,
        )

    query_cur, cotan_cur, lse_cur, delta_cur, query_acc, key_acc, value_acc = lax.fori_loop(
        0, nblocks - 1, cycle_step, start
    )
    query_part, key_part, value_part = crop_terms(
        query_cur, cotan_cur, lse_cur, delta_cur, key_h, value_h
    )
    query_total = shifted((query_acc + query_part).astype(jnp.bfloat16), "blk", 1).astype(
        jnp.float32
    )
    grad_q16 = (query_total * SCALING).astype(jnp.bfloat16)
    grad_k16 = ((key_acc + key_part) * SCALING).astype(jnp.bfloat16)
    grad_v16 = (value_acc + value_part).astype(jnp.bfloat16)
    return tuple(
        lax.all_to_all(grad, "head", split_axis=1, concat_axis=2, tiled=True)
        for grad in (grad_q16, grad_k16, grad_v16)
    )


def call(kernel, out_shape, *operands, scratch=(), remote=0, out_space=pltpu.VMEM, limit=VMEM_LIMIT):
    specs = [
        pl.BlockSpec(memory_space=pltpu.HBM if i < remote else pltpu.VMEM)
        for i in range(len(operands))
    ]
    return pl.pallas_call(
        kernel,
        out_shape=out_shape,
        in_specs=specs,
        out_specs=jax.tree.map(lambda _: pl.BlockSpec(memory_space=out_space), out_shape),
        scratch_shapes=list(scratch),
        compiler_params=pltpu.CompilerParams(vmem_limit_bytes=limit),
    )(*operands)


def place():
    h, b = lax.axis_index("head"), lax.axis_index("blk")
    return lax.div(h, 2), lax.rem(lax.div(b, 2), 2), lax.rem(h, 2), h


def shape(*dims, dtype=BF16):
    return jax.ShapeDtypeStruct(dims, dtype)


def head_of(array, head):
    return array[:, HDIM * head : HDIM * (head + 1)]


def pieces_of(row):
    high = row.astype(BF16)
    rest = row - high.astype(F32)
    middle = rest.astype(BF16)
    low = (rest - middle.astype(F32)).astype(BF16)
    return jnp.concatenate([high.astype(F32), middle.astype(F32), low.astype(F32)], axis=0)


def pack_inputs_kernel(
    q_in, k_in, v_in, o_in, do_in, lse_in, out0, out1, out2, out3,
    q_s, k_s, v_s, o_s, do_s, lse_s, out_ref, done, sent,
):
    x, w, c, _ = place()
    copies = [
        pltpu.make_async_copy(source, target, done.at[i])
        for i, (source, target) in enumerate(
            ((do_in, do_s), (o_in, o_s), (lse_in, lse_s), (q_in, q_s), (k_in, k_s), (v_in, v_s))
        )
    ]
    for copy in copies:
        copy.start()
    rows = q_s.shape[0]
    for copy in copies[:3]:
        copy.wait()
    products = do_s[...].astype(F32) * o_s[...].astype(F32)
    deltas = jnp.concatenate(
        [jnp.sum(head_of(products, head), axis=1, keepdims=True) for head in range(8)], axis=1
    ).T
    lse = lse_s[pl.ds(1 - w, 1), :] * LOG2E
    lse = jnp.concatenate([lse[:, rows * i : rows * (i + 1)] for i in range(4)], axis=0)
    lse = pieces_of(lse)
    for copy in copies[3:]:
        copy.wait()
    q, k, v, do = q_s[...], k_s[...], v_s[...], do_s[...]
    blank = jnp.zeros((3, 128 - rows), F32)
    gap = jnp.zeros((5, 128), F32)
    edge = jnp.zeros((8, 128 - rows), F32)
    side_lse = [
        jnp.concatenate([lse[0:8], edge], axis=1),
        jnp.concatenate([jnp.concatenate([lse[8:12], lse[8:12]], axis=0), edge], axis=1),
    ]
    for side in range(2):

        @pl.when(c == side)
        def _():
            for xs in range(2):
                for ws in range(2):
                    near, deep, spots = [], [], []
                    for i, cs in enumerate((side, 1 - side)):
                        head = 4 * xs + 2 * cs + ws
                        value = head_of(v, head)
                        near += [head_of(q, head), head_of(do, head), head_of(k, head), value[:, :16]]
                        deep.append(value[:, 16:])
                        delta = jnp.concatenate([pieces_of(deltas[head : head + 1, :]), blank], axis=1)
                        spots += [jnp.concatenate([delta, gap], axis=0), side_lse[i]]
                    j = 2 * (x ^ xs) + (w ^ ws)
                    out_ref[j, 0:rows] = jnp.concatenate(near + deep, axis=1)
                    below = jnp.concatenate(spots + [jnp.zeros((8, 128), F32)], axis=1)
                    out_ref[j, rows:PADDED] = below.astype(BF16)

    copies = [
        pltpu.make_async_copy(out_ref.at[j], out, sent.at[j])
        for j, out in enumerate((out0, out1, out2, out3))
    ]
    for copy in copies:
        copy.start()
    for copy in copies:
        copy.wait()


def parts_of(own, near, other, j, r):
    if r:
        return other[j], 320
    return (own if j == 0 else near[j - 1])[...], 512


def gather_queries_kernel(own, near1, near2, near3, other, lse_in, low, high, lse_s):
    rows = PADDED - 8
    near = (near1, near2, near3)
    _, w, _, h = place()
    lse_own = lse_in[pl.ds(w, 1), :] * LOG2E
    below = near1[rows:PADDED, :].astype(F32)
    lse_near = below[0:4, 128 : 128 + rows] + below[4:8, 128 : 128 + rows]
    lse_near = lse_near + below[0:4, 384 : 384 + rows]
    lse_s[...] = jnp.concatenate(
        [lse_own[:, rows * i : rows * (i + 1)] for i in range(4)] + [lse_near], axis=0
    )
    blocks, spots = [], []
    gap = jnp.zeros((6, PADDED - rows), F32)
    for j in range(4):
        for r in range(2):
            held, _ = parts_of(own, near, other, j, r)
            blocks.append(held[0:rows, 0:160])
            delta = held[rows:PADDED, 0:128].astype(F32)[0:3, 0:rows]
            lse = lse_s[pl.ds(4 * (j % 2) + (h ^ (2 * (j // 2) + r)), 1), :]
            spots += [jnp.concatenate([delta, pieces_of(lse)], axis=0), gap]
    for at, wire in ((0, low), (4, high)):
        wire[0:rows] = jnp.concatenate(blocks[at : at + 4], axis=1)
        below = jnp.concatenate(spots[2 * at : 2 * at + 8] + [jnp.zeros((6, 256), F32)], axis=1)
        below = jnp.concatenate([below, jnp.zeros((2, 640), F32)], axis=0)
        wire[rows:PADDED] = below.astype(BF16)


def gather_keys_kernel(own, near1, near2, near3, other, wide):
    rows = wide.shape[0]
    blocks = []
    for j in range(4):
        for r in range(2):
            held, deep = parts_of(own, (near1, near2, near3), other, j, r)
            blocks += [held[0:rows, 160:256], held[0:rows, deep : deep + 64]]
    wide[...] = jnp.concatenate(blocks, axis=1)


def rows_of(wires):
    rows = PADDED - 8
    below = jnp.concatenate(
        [wire[rows:PADDED, 0 : 4 * PADDED].astype(F32) for wire in wires], axis=1
    )
    return below[3:4] + below[4:5] + below[5:6], below[0:1] + below[1:2] + below[2:3]


def spread(wide, left, right, first=0):
    rows = PADDED - 8
    blank = jnp.zeros((16, HDIM), BF16)
    for i in range(wide.shape[1] // (2 * HDIM)):
        at, lane = PADDED * (first + i), 2 * HDIM * i
        for target, start in ((left, lane), (right, lane + HDIM)):
            target[pl.ds(at + PADDED - 16, 16), :] = blank
            target[pl.ds(at, rows), :] = wide[0:rows, start : start + HDIM]


def tile_step(q, do, k_s, v_s, lse, delta, chunk=384):
    q_t, do_t = q.T, do.T
    k_t = k_s[...].T
    dq_t = None
    parts = []
    for start in range(0, k_s.shape[0], chunk):
        spot = slice(start, start + chunk)
        k, v = k_s[spot, :], v_s[spot, :]
        scores = jnp.dot(k, q_t, preferred_element_type=F32)
        probs = jnp.exp2(scores * (SCALING * LOG2E) - lse)
        dv = jnp.dot(probs.astype(BF16), do, preferred_element_type=F32)
        dprobs = jnp.dot(v, do_t, preferred_element_type=F32)
        dscores = (probs * (dprobs - delta)).astype(BF16)
        dk = jnp.dot(dscores, q, preferred_element_type=F32)
        more = jnp.dot(k_t[:, spot], dscores, preferred_element_type=F32)
        dq_t = more if dq_t is None else dq_t + more
        parts.append((spot, dk, dv))
    return dq_t, parts


def to_wire(arrays, rows):
    count = arrays[0].shape[0] // PADDED
    return jnp.concatenate(
        [a[PADDED * i : PADDED * i + rows].astype(BF16) for i in range(count) for a in arrays],
        axis=1,
    )


def own_own_kernel(low, high, keys, dq_t, dk, dv, q_s, do_s, k_s, v_s):
    spread(low, q_s, do_s)
    spread(high, q_s, do_s, 4)
    spread(keys, k_s, v_s)
    dq_t[...], parts = tile_step(q_s[...], do_s[...], k_s, v_s, *rows_of([low, high]))
    for spot, dk_part, dv_part in parts:
        dk[spot, :] = dk_part
        dv[spot, :] = dv_part


def own_far_kernel(low, high, q_s, do_s, keys, dq_before, dq_t, dk, dv, k_s, v_s):
    spread(keys, k_s, v_s)
    more, parts = tile_step(q_s[...], do_s[...], k_s, v_s, *rows_of([low, high]))
    dq_t[...] = dq_before[...] + more
    for spot, dk_part, dv_part in parts:
        dk[spot, :] = dk_part
        dv[spot, :] = dv_part


def low_kernel(
    low, k_far, v_far, k_own, v_own, dk_far_in, dv_far_in, dk_own_in, dv_own_in,
    dq_t, dk_far, dv_far, dk_own, dv_own, q_s, do_s,
):
    spread(low, q_s, do_s)
    q, do = q_s[...], do_s[...]
    lse, delta = rows_of([low])
    total = None
    for k_s, v_s, dk_in, dv_in, dk, dv in (
        (k_far, v_far, dk_far_in, dv_far_in, dk_far, dv_far),
        (k_own, v_own, dk_own_in, dv_own_in, dk_own, dv_own),
    ):
        more, parts = tile_step(q, do, k_s, v_s, lse, delta)
        total = more if total is None else total + more
        for spot, dk_part, dv_part in parts:
            dk[spot, :] = dk_in[spot, :] + dk_part
            dv[spot, :] = dv_in[spot, :] + dv_part
    dq_t[...] = total


def high_far_kernel(high, k_far, v_far, dk_in, dv_in, dq_t, wire, q_s, do_s, dk, dv):
    spread(high, q_s, do_s)
    dq_t[...], parts = tile_step(q_s[...], do_s[...], k_far, v_far, *rows_of([high]))
    for spot, dk_part, dv_part in parts:
        dk[spot, :] = (dk_in[spot, :] + dk_part) * SCALING
        dv[spot, :] = dv_in[spot, :] + dv_part
    wire[...] = to_wire([dk[...], dv[...]], wire.shape[0])


def high_own_kernel(
    high, q_s, do_s, k_own, v_own, dq_low, dq_high, dk_in, dv_in, wire, dk, dv
):
    more, parts = tile_step(q_s[...], do_s[...], k_own, v_own, *rows_of([high]))
    dq = jnp.concatenate([dq_low[...], dq_high[...] + more], axis=1) * SCALING
    wire[...] = to_wire([dq.T], wire.shape[0])
    for spot, dk_part, dv_part in parts:
        dk[spot, :] = dk_in[spot, :] + dk_part
        dv[spot, :] = dv_in[spot, :] + dv_part


def own_grads_kernel(dq_t, dk, dv, out):
    rows = out.shape[1]
    dq = dq_t[...].T * SCALING
    zeros = jnp.zeros((rows, 16), F32)
    for i in range(8):
        spot = slice(PADDED * i, PADDED * i + rows)
        block = jnp.concatenate([dq[spot], dk[spot, :] * SCALING, dv[spot, :], zeros], axis=1)
        out[i // 2, :, 256 * (i % 2) : 256 * (i % 2) + 256] = block


def pack_grads_kernel(own, dkv_wire, dq_wire, out):
    rows = dkv_wire.shape[0]
    dq = dq_wire[...]
    dkv = dkv_wire[...]
    zeros = jnp.zeros((rows, 16), BF16)
    for i in range(8):
        block = jnp.concatenate(
            [
                dq[:, HDIM * i : HDIM * (i + 1)],
                dkv[:, 2 * HDIM * i : 2 * HDIM * (i + 1)],
                zeros,
            ],
            axis=1,
        )
        lanes = slice(256 * (i % 2), 256 * (i % 2) + 256)
        out[i // 2, :, lanes] = (own[i // 2, :, lanes] + block.astype(F32)).astype(BF16)


def unpack_grads_kernel(held, other, dq, dk, dv):
    x, w, c, _ = place()
    blocks = []
    for head in range(8):
        xs, cs, ws = head // 4, (head // 2) % 2, head % 2
        j = 2 * (x ^ xs) + (w ^ ws)
        blocks.append(
            jnp.where(c == cs, held[j][:, :256].astype(F32), other[j].astype(F32))
        )
    for k, out in enumerate((dq, dk, dv)):
        out[...] = jnp.concatenate(
            [block[:, HDIM * k : HDIM * (k + 1)] for block in blocks], axis=1
        ).astype(BF16)


def flipped(array, head_bits, blk_bits):
    heads, blks = lax.axis_size("head"), lax.axis_size("blk")
    if not blk_bits:
        return lax.ppermute(array, "head", [(i, i ^ head_bits) for i in range(heads)])
    if not head_bits:
        return lax.ppermute(array, "blk", [(i, i ^ blk_bits) for i in range(blks)])
    bits = head_bits * blks + blk_bits
    return lax.ppermute(array, ("head", "blk"), [(i, i ^ bits) for i in range(heads * blks)])


def to_chips(packed):
    return [flipped(packed[1], 0, 2), flipped(packed[2], 2, 0), flipped(packed[3], 2, 2)]


def grid_body(queries, keys, values, outputs, grad_out, lse):
    rows = queries.shape[1]
    padded = 8 * PADDED
    half = padded // 2

    packed = call(
        pack_inputs_kernel,
        (shape(PADDED, 640),) * 4,
        queries[0], keys[0], values[0], outputs[0], grad_out[0], lse[0],
        remote=6,
        out_space=pltpu.HBM,
        limit=57 * 1024 * 1024,
        scratch=[pltpu.VMEM(queries.shape[1:], BF16)] * 5
        + [pltpu.VMEM(lse.shape[1:], F32), pltpu.VMEM((4, PADDED, 640), BF16)]
        + [pltpu.SemaphoreType.DMA((6,)), pltpu.SemaphoreType.DMA((4,))],
    )
    own = packed[0]
    near = to_chips(packed)
    other = flipped(jnp.stack([a[:, 256:] for a in [own] + near]), 1, 0)
    low, high = call(
        gather_queries_kernel,
        (shape(PADDED, 640), shape(PADDED, 640)),
        own, *near, other, lse[0],
        scratch=[pltpu.VMEM((8, rows), F32)],
    )
    low_far = flipped(low, 0, 4)
    other, low = lax.optimization_barrier((other, low))
    k_wide = call(gather_keys_kernel, shape(rows, 1280), own, *near, other)
    k_wide_far = flipped(k_wide, 0, 1)

    grad = shape(padded, HDIM, dtype=F32)
    side = shape(padded, HDIM)
    dq_shape = shape(HDIM, padded, dtype=F32)
    dq_own, dk_own, dv_own, q_s, do_s, k_own, v_own = call(
        own_own_kernel, (dq_shape, grad, grad, side, side, side, side), low, high, k_wide
    )
    high, dq_own = lax.optimization_barrier((high, dq_own))
    high_far = flipped(high, 0, 4)
    dq_own, dk_far, dv_far, k_far, v_far = call(
        own_far_kernel, (dq_shape, grad, grad, side, side), low, high, q_s, do_s, k_wide_far, dq_own
    )
    dq_low, dk_far, dv_far, dk_own, dv_own = call(
        low_kernel, (shape(HDIM, half, dtype=F32), grad, grad, grad, grad),
        low_far, k_far, v_far, k_own, v_own, dk_far, dv_far, dk_own, dv_own,
        scratch=[pltpu.VMEM((half, HDIM), BF16)] * 2,
    )
    few = shape(half, HDIM)
    dq_high, dkv_wire, q_s, do_s = call(
        high_far_kernel,
        (shape(HDIM, half, dtype=F32), shape(rows, 1280), few, few),
        high_far, k_far, v_far, dk_far, dv_far,
        scratch=[pltpu.VMEM((padded, HDIM), F32)] * 2,
    )
    dkv_back = flipped(dkv_wire, 0, 1)
    dq_wire, dk_own, dv_own = call(
        high_own_kernel, (shape(rows, 640), grad, grad),
        high_far, q_s, do_s, k_own, v_own, dq_low, dq_high, dk_own, dv_own,
    )
    dq_back = flipped(dq_wire, 0, 4)
    own_g = call(own_grads_kernel, shape(4, rows, 512, dtype=F32), dq_own, dk_own, dv_own)
    packed_g = call(pack_grads_kernel, shape(4, rows, 512), own_g, dkv_back, dq_back)
    held = jnp.stack([packed_g[0]] + to_chips(packed_g))
    other = flipped(held[:, :, 256:], 1, 0)
    out = shape(rows, queries.shape[2])
    grads = call(unpack_grads_kernel, (out, out, out), held, other)
    return tuple(grad[None] for grad in grads)


def solution(mesh):
    placed = P(None, ("blk", "head"), None)
    on_grid = mesh.shape["head"] == 4 and mesh.shape["blk"] == 8
    return jax.shard_map(
        grid_body if on_grid else ring_body,
        mesh=mesh,
        in_specs=(placed,) * 5 + (P(None, "head", "blk"),),
        out_specs=(placed,) * 3,
        check_vma=False,
    )
```

```python
import functools
import math

import jax
import jax.numpy as jnp
from jax import lax
from jax.experimental import pallas as pl
from jax.experimental.pallas import tpu as pltpu
from jax.sharding import PartitionSpec as P

HDIM = 80
SCALING = HDIM ** (-0.5)
LOG2E = math.log2(math.e)
PADDED = 96
VMEM_LIMIT = 24 * 1024 * 1024
F32 = jnp.float32
BF16 = jnp.bfloat16


def shifted(block, axis, distance):
    devices = range(lax.axis_size(axis))
    route = [((i - distance) % len(devices), i) for i in devices]
    return lax.ppermute(block, axis, route)


def tile_terms(query_h, cotan_h, lse_rows, delta_rows, key_h, value_h):
    query_rows = query_h.shape[0]
    key_rows = key_h.shape[0]
    groups = query_h.shape[1]
    scores = (
        jnp.einsum("qhd,khd->hqk", query_h, key_h, preferred_element_type=jnp.float32) * SCALING
    )
    probs = jnp.exp(scores - lse_rows[:, :, None])
    probs16 = probs.astype(jnp.bfloat16)
    value_part = jnp.einsum("hqk,qhd->khd", probs16, cotan_h, preferred_element_type=jnp.float32)
    dprobs = jnp.einsum("qhd,khd->hqk", cotan_h, value_h, preferred_element_type=jnp.float32)
    dscores = (probs * (dprobs - delta_rows[:, :, None])).astype(jnp.bfloat16)
    query_part = jnp.einsum("hqk,khd->qhd", dscores, key_h, preferred_element_type=jnp.float32)
    key_part = jnp.einsum("hqk,qhd->khd", dscores, query_h, preferred_element_type=jnp.float32)
    return (
        query_part.reshape(query_rows, groups * HDIM),
        key_part.reshape(key_rows, groups * HDIM),
        value_part.reshape(key_rows, groups * HDIM),
    )


def crop_terms(query_h, cotan_h, lse_rows, delta_rows, key_h, value_h):
    return lax.map(
        lambda pieces: tile_terms(*pieces), (query_h, cotan_h, lse_rows, delta_rows, key_h, value_h)
    )


def ring_body(queries, keys, values, outputs, grad_out, lse):
    crops = queries.shape[0]
    groups = lse.shape[1]
    rows = lse.shape[2]
    query_own, key_own, value_own, cotan_own, output_own = (
        lax.all_to_all(sent, "head", split_axis=2, concat_axis=1, tiled=True)
        for sent in (queries, keys, values, grad_out, outputs)
    )
    products = cotan_own.astype(jnp.float32) * output_own.astype(jnp.float32)
    delta_rows = jnp.transpose(
        jnp.sum(products.reshape(crops, rows, groups, HDIM), axis=-1), (0, 2, 1)
    )
    query_h = query_own.reshape(crops, rows, groups, HDIM)
    cotan_h = cotan_own.reshape(crops, rows, groups, HDIM)
    key_h = key_own.reshape(crops, rows, groups, HDIM)
    value_h = value_own.reshape(crops, rows, groups, HDIM)
    width = groups * HDIM
    nblocks = lax.axis_size("blk")
    zeros_acc = jnp.zeros((crops, rows, width), jnp.float32)
    start = (query_h, cotan_h, lse, delta_rows, zeros_acc, zeros_acc, zeros_acc)

    def cycle_step(index, carry):
        query_cur, cotan_cur, lse_cur, delta_cur, query_acc, key_acc, value_acc = carry
        query_part, key_part, value_part = crop_terms(
            query_cur, cotan_cur, lse_cur, delta_cur, key_h, value_h
        )
        query_acc, lse_cur, delta_cur = shifted(
            (query_acc + query_part, lse_cur, delta_cur), "blk", 1
        )
        query_cur, cotan_cur = shifted((query_cur, cotan_cur), "blk", 1)
        return (
            query_cur,
            cotan_cur,
            lse_cur,
            delta_cur,
            query_acc,
            key_acc + key_part,
            value_acc + value_part,
        )

    query_cur, cotan_cur, lse_cur, delta_cur, query_acc, key_acc, value_acc = lax.fori_loop(
        0, nblocks - 1, cycle_step, start
    )
    query_part, key_part, value_part = crop_terms(
        query_cur, cotan_cur, lse_cur, delta_cur, key_h, value_h
    )
    query_total = shifted((query_acc + query_part).astype(jnp.bfloat16), "blk", 1).astype(
        jnp.float32
    )
    grad_q16 = (query_total * SCALING).astype(jnp.bfloat16)
    grad_k16 = ((key_acc + key_part) * SCALING).astype(jnp.bfloat16)
    grad_v16 = (value_acc + value_part).astype(jnp.bfloat16)
    return tuple(
        lax.all_to_all(grad, "head", split_axis=1, concat_axis=2, tiled=True)
        for grad in (grad_q16, grad_k16, grad_v16)
    )


def call(kernel, out_shape, *operands, scratch=(), remote=0, flops=0, out_space=pltpu.VMEM, limit=VMEM_LIMIT):
    specs = [
        pl.BlockSpec(memory_space=pltpu.HBM if i < remote else pltpu.VMEM)
        for i in range(len(operands))
    ]
    return pl.pallas_call(
        kernel,
        out_shape=out_shape,
        in_specs=specs,
        out_specs=jax.tree.map(lambda _: pl.BlockSpec(memory_space=out_space), out_shape),
        scratch_shapes=list(scratch),
        cost_estimate=pl.CostEstimate(flops=flops, bytes_accessed=0, transcendentals=0) if flops else None,
        compiler_params=pltpu.CompilerParams(vmem_limit_bytes=limit),
    )(*operands)


def place():
    h, b = lax.axis_index("head"), lax.axis_index("blk")
    return lax.div(h, 2), lax.rem(lax.div(b, 2), 2), lax.rem(h, 2), h


def shape(*dims, dtype=BF16):
    return jax.ShapeDtypeStruct(dims, dtype)


def head_of(array, head):
    return array[:, HDIM * head : HDIM * (head + 1)]


def pieces_of(row):
    high = row.astype(BF16)
    rest = row - high.astype(F32)
    middle = rest.astype(BF16)
    low = (rest - middle.astype(F32)).astype(BF16)
    return jnp.concatenate([high.astype(F32), middle.astype(F32), low.astype(F32)], axis=0)


def pack_inputs_kernel(
    q_in, k_in, v_in, o_in, do_in, lse_in, out0, out1, out2, out3,
    q_s, k_s, v_s, o_s, do_s, lse_s, out_ref, done, sent,
):
    x, w, c, _ = place()
    copies = [
        pltpu.make_async_copy(source, target, done.at[i])
        for i, (source, target) in enumerate(
            ((q_in, q_s), (k_in, k_s), (v_in, v_s), (do_in, do_s), (o_in, o_s), (lse_in, lse_s))
        )
    ]
    for copy in copies:
        copy.start()
    for copy in copies:
        copy.wait()
    rows = q_s.shape[0]
    q, k, v, do = q_s[...], k_s[...], v_s[...], do_s[...]
    outs = (out0, out1, out2, out3)

    def leave(part, spot):
        return [
            pltpu.make_async_copy(out_ref.at[j, spot], out.at[spot], sent.at[4 * part + j])
            for j, out in enumerate(outs)
        ]

    for side in range(2):

        @pl.when(c == side)
        def _():
            for xs in range(2):
                for ws in range(2):
                    near, deep = [], []
                    for cs in (side, 1 - side):
                        head = 4 * xs + 2 * cs + ws
                        value = head_of(v, head)
                        near += [head_of(q, head), head_of(do, head), head_of(k, head), value[:, :16]]
                        deep.append(value[:, 16:])
                    j = 2 * (x ^ xs) + (w ^ ws)
                    out_ref[j, 0:rows] = jnp.concatenate(near + deep, axis=1)

    most = leave(0, pl.ds(0, PADDED - 16))
    for copy in most:
        copy.start()
    products = do.astype(F32) * o_s[...].astype(F32)
    high = products.astype(BF16)
    rest = products - high.astype(F32)
    middle = rest.astype(BF16)
    low = (rest - middle.astype(F32)).astype(BF16)
    row = lax.broadcasted_iota(jnp.int32, (8, 640), 0)
    lane = lax.broadcasted_iota(jnp.int32, (8, 640), 1)
    mine = jnp.where((lane >= HDIM * row) & (lane < HDIM * (row + 1)), 1.0, 0.0).astype(BF16)
    deltas = sum(
        lax.dot_general(mine, part, (((1,), (1,)), ((), ())), preferred_element_type=F32)
        for part in (low, middle, high)
    )
    lse = lse_s[pl.ds(1 - w, 1), :] * LOG2E
    lse = jnp.concatenate([lse[:, rows * i : rows * (i + 1)] for i in range(4)], axis=0)
    lse = pieces_of(lse)
    blank = jnp.zeros((3, 128 - rows), F32)
    gap = jnp.zeros((5, 128), F32)
    edge = jnp.zeros((8, 128 - rows), F32)
    sides = [
        jnp.concatenate([lse[0:8], edge], axis=1),
        jnp.concatenate([jnp.concatenate([lse[8:12], lse[8:12]], axis=0), edge], axis=1),
    ]
    for xs in range(2):
        for ws in range(2):
            j = 2 * (x ^ xs) + (w ^ ws)
            pair = []
            for cs in range(2):
                head = 4 * xs + 2 * cs + ws
                delta = jnp.concatenate([pieces_of(deltas[head : head + 1, :]), blank], axis=1)
                pair.append(jnp.concatenate([delta, gap], axis=0))
            kept = jnp.where(c == 0, pair[0], pair[1])
            given = jnp.where(c == 0, pair[1], pair[0])
            spots = [kept, sides[0], given, sides[1], jnp.zeros((8, 128), F32)]
            out_ref[j, rows:PADDED] = jnp.concatenate(spots, axis=1).astype(BF16)
    last = leave(1, pl.ds(PADDED - 16, 16))
    for copy in last:
        copy.start()
    for copy in most + last:
        copy.wait()


def parts_of(own, near, other, j, r):
    if r:
        return other[j], 320
    return (own if j == 0 else near[j - 1])[...], 512


def gather_queries_kernel(own, near1, near2, near3, other0, other1, other2, other3, lse_in, low, high, lse_s):
    other = (other0, other1, other2, other3)
    rows = PADDED - 8
    near = (near1, near2, near3)
    _, w, _, h = place()
    lse_own = lse_in[pl.ds(w, 1), :] * LOG2E
    below = near1[rows:PADDED, :].astype(F32)
    lse_near = below[0:4, 128 : 128 + rows] + below[4:8, 128 : 128 + rows]
    lse_near = lse_near + below[0:4, 384 : 384 + rows]
    lse_s[...] = jnp.concatenate(
        [lse_own[:, rows * i : rows * (i + 1)] for i in range(4)] + [lse_near], axis=0
    )
    blocks, spots = [], []
    gap = jnp.zeros((6, PADDED - rows), F32)
    for j in range(4):
        for r in range(2):
            held, _ = parts_of(own, near, other, j, r)
            blocks.append(held[0:rows, 0:160])
            delta = held[rows:PADDED, 0:128].astype(F32)[0:3, 0:rows]
            lse = lse_s[pl.ds(4 * (j % 2) + (h ^ (2 * (j // 2) + r)), 1), :]
            spots += [jnp.concatenate([delta, pieces_of(lse)], axis=0), gap]
    for at, wire in ((0, low), (4, high)):
        wire[0:rows] = jnp.concatenate(blocks[at : at + 4], axis=1)
        below = jnp.concatenate(spots[2 * at : 2 * at + 8] + [jnp.zeros((6, 256), F32)], axis=1)
        below = jnp.concatenate([below, jnp.zeros((2, 640), F32)], axis=0)
        wire[rows:PADDED] = below.astype(BF16)


def gather_keys_kernel(own, near1, near2, near3, other0, other1, other2, other3, low, high):
    other = (other0, other1, other2, other3)
    rows = low.shape[0]
    blocks = []
    for j in range(4):
        for r in range(2):
            held, deep = parts_of(own, (near1, near2, near3), other, j, r)
            blocks += [held[0:rows, 160:256], held[0:rows, deep : deep + 64]]
    low[...] = jnp.concatenate(blocks[:8], axis=1)
    high[...] = jnp.concatenate(blocks[8:], axis=1)


def rows_of(wires):
    rows = PADDED - 8
    below = jnp.concatenate(
        [wire[rows:PADDED, 0 : 4 * PADDED].astype(F32) for wire in wires], axis=1
    )
    return below[3:4] + below[4:5] + below[5:6], below[0:1] + below[1:2] + below[2:3]


def spread(wide, left, right, first=0):
    rows = PADDED - 8
    blank = jnp.zeros((16, HDIM), BF16)
    for i in range(wide.shape[1] // (2 * HDIM)):
        at, lane = PADDED * (first + i), 2 * HDIM * i
        for target, start in ((left, lane), (right, lane + HDIM)):
            target[pl.ds(at + PADDED - 16, 16), :] = blank
            target[pl.ds(at, rows), :] = wide[0:rows, start : start + HDIM]


def tile_step(q, do, k_s, v_s, lse, delta, chunk=384):
    q_t, do_t = q.T, do.T
    k_t = k_s[...].T
    dq_t = None
    parts = []
    for start in range(0, k_s.shape[0], chunk):
        spot = slice(start, start + chunk)
        k, v = k_s[spot, :], v_s[spot, :]
        scores = jnp.dot(k, q_t, preferred_element_type=F32)
        probs = jnp.exp2(scores * (SCALING * LOG2E) - lse)
        dv = jnp.dot(probs.astype(BF16), do, preferred_element_type=F32)
        dprobs = jnp.dot(v, do_t, preferred_element_type=F32)
        dscores = (probs * (dprobs - delta)).astype(BF16)
        dk = jnp.dot(dscores, q, preferred_element_type=F32)
        more = jnp.dot(k_t[:, spot], dscores, preferred_element_type=F32)
        dq_t = more if dq_t is None else dq_t + more
        parts.append((spot, dk, dv))
    return dq_t, parts


def to_wire(arrays, rows):
    count = arrays[0].shape[0] // PADDED
    return jnp.concatenate(
        [a[PADDED * i : PADDED * i + rows].astype(BF16) for i in range(count) for a in arrays],
        axis=1,
    )


def own_own_kernel(low, high, k_low, k_high, dq_t, dk, dv, q_s, do_s, k_s, v_s):
    spread(low, q_s, do_s)
    spread(high, q_s, do_s, 4)
    spread(k_low, k_s, v_s)
    spread(k_high, k_s, v_s, 4)
    dq_t[...], parts = tile_step(q_s[...], do_s[...], k_s, v_s, *rows_of([low, high]))
    for spot, dk_part, dv_part in parts:
        dk[spot, :] = dk_part
        dv[spot, :] = dv_part


def own_far_kernel(low, high, q_s, do_s, k_low, k_high, dq_before, dq_t, dk, dv, k_s, v_s):
    spread(k_low, k_s, v_s)
    spread(k_high, k_s, v_s, 4)
    more, parts = tile_step(q_s[...], do_s[...], k_s, v_s, *rows_of([low, high]))
    dq_t[...] = dq_before[...] + more
    for spot, dk_part, dv_part in parts:
        dk[spot, :] = dk_part
        dv[spot, :] = dv_part


def low_kernel(
    low, k_far, v_far, k_own, v_own, dk_far_in, dv_far_in, dk_own_in, dv_own_in,
    dq_t, dk_far, dv_far, dk_own, dv_own, q_s, do_s,
):
    spread(low, q_s, do_s)
    q, do = q_s[...], do_s[...]
    lse, delta = rows_of([low])
    total = None
    for k_s, v_s, dk_in, dv_in, dk, dv in (
        (k_far, v_far, dk_far_in, dv_far_in, dk_far, dv_far),
        (k_own, v_own, dk_own_in, dv_own_in, dk_own, dv_own),
    ):
        more, parts = tile_step(q, do, k_s, v_s, lse, delta)
        total = more if total is None else total + more
        for spot, dk_part, dv_part in parts:
            dk[spot, :] = dk_in[spot, :] + dk_part
            dv[spot, :] = dv_in[spot, :] + dv_part
    dq_t[...] = total


def high_far_kernel(high, k_far, v_far, dk_in, dv_in, dq_t, wire, q_s, do_s, dk, dv):
    spread(high, q_s, do_s)
    dq_t[...], parts = tile_step(q_s[...], do_s[...], k_far, v_far, *rows_of([high]))
    for spot, dk_part, dv_part in parts:
        dk[spot, :] = (dk_in[spot, :] + dk_part) * SCALING
        dv[spot, :] = dv_in[spot, :] + dv_part
    wire[...] = to_wire([dk[...], dv[...]], wire.shape[0])


def high_own_kernel(
    high, q_s, do_s, k_own, v_own, dq_low, dq_high, dk_in, dv_in, wire, dk, dv
):
    more, parts = tile_step(q_s[...], do_s[...], k_own, v_own, *rows_of([high]))
    dq = jnp.concatenate([dq_low[...], dq_high[...] + more], axis=1) * SCALING
    wire[...] = to_wire([dq.T], wire.shape[0])
    for spot, dk_part, dv_part in parts:
        dk[spot, :] = dk_in[spot, :] + dk_part
        dv[spot, :] = dv_in[spot, :] + dv_part


def own_grads_kernel(dq_t, dk, dv, out):
    rows = out.shape[1]
    dq = dq_t[...].T * SCALING
    zeros = jnp.zeros((rows, 16), F32)
    for i in range(8):
        spot = slice(PADDED * i, PADDED * i + rows)
        block = jnp.concatenate([dq[spot], dk[spot, :] * SCALING, dv[spot, :], zeros], axis=1)
        out[i // 2, :, 256 * (i % 2) : 256 * (i % 2) + 256] = block


def pack_grads_kernel(own, dkv_wire, dq_wire, out):
    rows = dkv_wire.shape[0]
    dq = dq_wire[...]
    dkv = dkv_wire[...]
    zeros = jnp.zeros((rows, 16), BF16)
    for i in range(8):
        block = jnp.concatenate(
            [
                dq[:, HDIM * i : HDIM * (i + 1)],
                dkv[:, 2 * HDIM * i : 2 * HDIM * (i + 1)],
                zeros,
            ],
            axis=1,
        )
        lanes = slice(256 * (i % 2), 256 * (i % 2) + 256)
        out[i // 2, :, lanes] = (own[i // 2, :, lanes] + block.astype(F32)).astype(BF16)


def unpack_grads_kernel(*refs):
    kept, given, dq, dk, dv, held, other = refs[0:4], refs[4:8], *refs[8:]
    x, w, c, _ = place()
    for j in range(4):
        held[j] = kept[j][:, 0:256]
        other[j] = given[j][...]
    blocks = []
    for head in range(8):
        xs, cs, ws = head // 4, (head // 2) % 2, head % 2
        j = 2 * (x ^ xs) + (w ^ ws)
        blocks.append(jnp.where(c == cs, held[j].astype(F32), other[j].astype(F32)).astype(BF16))
    for k, out in enumerate((dq, dk, dv)):
        out[...] = jnp.concatenate(
            [block[:, HDIM * k : HDIM * (k + 1)] for block in blocks], axis=1
        )


def flipped(array, head_bits, blk_bits):
    heads, blks = lax.axis_size("head"), lax.axis_size("blk")
    if not blk_bits:
        return lax.ppermute(array, "head", [(i, i ^ head_bits) for i in range(heads)])
    if not head_bits:
        return lax.ppermute(array, "blk", [(i, i ^ blk_bits) for i in range(blks)])
    bits = head_bits * blks + blk_bits
    return lax.ppermute(array, ("head", "blk"), [(i, i ^ bits) for i in range(heads * blks)])


def to_chips(packed):
    return [flipped(packed[1], 0, 2), flipped(packed[2], 2, 0), flipped(packed[3], 2, 2)]


def grid_body(queries, keys, values, outputs, grad_out, lse):
    rows = queries.shape[1]
    padded = 8 * PADDED
    half = padded // 2

    packed = call(
        pack_inputs_kernel,
        (shape(PADDED, 640),) * 4,
        queries[0], keys[0], values[0], outputs[0], grad_out[0], lse[0],
        remote=6,
        out_space=pltpu.HBM,
        limit=57 * 1024 * 1024,
        scratch=[pltpu.VMEM(queries.shape[1:], BF16)] * 5
        + [pltpu.VMEM(lse.shape[1:], F32), pltpu.VMEM((4, PADDED, 640), BF16)]
        + [pltpu.SemaphoreType.DMA((6,)), pltpu.SemaphoreType.DMA((8,))],
    )
    own = packed[0]
    near = to_chips(packed)
    other = [flipped(a[:, 256:], 1, 0) for a in [own] + near]
    low, high = call(
        gather_queries_kernel,
        (shape(PADDED, 640), shape(PADDED, 640)),
        own, *near, *other, lse[0],
        scratch=[pltpu.VMEM((8, rows), F32)],
    )
    low_far = flipped(low, 0, 4)
    other, low = lax.optimization_barrier((other, low))
    wires_k = call(gather_keys_kernel, (shape(rows, 640),) * 2, own, *near, *other)
    wires_k_far = [flipped(wire, 0, 1) for wire in wires_k]

    grad = shape(padded, HDIM, dtype=F32)
    side = shape(padded, HDIM)
    dq_shape = shape(HDIM, padded, dtype=F32)
    dq_own, dk_own, dv_own, q_s, do_s, k_own, v_own = call(
        own_own_kernel, (dq_shape, grad, grad, side, side, side, side), low, high, *wires_k
    )
    high, dq_own = lax.optimization_barrier((high, dq_own))
    high_far = flipped(high, 0, 4)
    dq_own, dk_far, dv_far, k_far, v_far = call(
        own_far_kernel, (dq_shape, grad, grad, side, side), low, high, q_s, do_s, *wires_k_far, dq_own
    )
    dq_low, dk_far, dv_far, dk_own, dv_own = call(
        low_kernel, (shape(HDIM, half, dtype=F32), grad, grad, grad, grad),
        low_far, k_far, v_far, k_own, v_own, dk_far, dv_far, dk_own, dv_own,
        flops=1000000000,
        scratch=[pltpu.VMEM((half, HDIM), BF16)] * 2,
    )
    few = shape(half, HDIM)
    dq_high, dkv_wire, q_s, do_s = call(
        high_far_kernel,
        (shape(HDIM, half, dtype=F32), shape(rows, 1280), few, few),
        high_far, k_far, v_far, dk_far, dv_far,
        scratch=[pltpu.VMEM((padded, HDIM), F32)] * 2,
    )
    dkv_back = flipped(dkv_wire, 0, 1)
    dq_wire, dk_own, dv_own = call(
        high_own_kernel, (shape(rows, 640), grad, grad),
        high_far, q_s, do_s, k_own, v_own, dq_low, dq_high, dk_own, dv_own,
    )
    dq_back = flipped(dq_wire, 0, 4)
    own_g = call(own_grads_kernel, shape(4, rows, 512, dtype=F32), dq_own, dk_own, dv_own)
    packed_g = call(pack_grads_kernel, shape(4, rows, 512), own_g, dkv_back, dq_back)
    held = [packed_g[0]] + to_chips(packed_g)
    other = [flipped(a[:, 256:], 1, 0) for a in held]
    out = shape(rows, queries.shape[2])
    grads = call(
        unpack_grads_kernel, (out, out, out), *held, *other,
        scratch=[pltpu.VMEM((4, rows, 256), BF16)] * 2,
    )
    return tuple(grad[None] for grad in grads)


def solution(mesh):
    placed = P(None, ("blk", "head"), None)
    on_grid = mesh.shape["head"] == 4 and mesh.shape["blk"] == 8
    return jax.shard_map(
        grid_body if on_grid else ring_body,
        mesh=mesh,
        in_specs=(placed,) * 5 + (P(None, "head", "blk"),),
        out_specs=(placed,) * 3,
        check_vma=False,
    )
```

```python
import functools
import math

import jax
import jax.numpy as jnp
from jax import lax
from jax.experimental import pallas as pl
from jax.experimental.pallas import tpu as pltpu
from jax.sharding import PartitionSpec as P

HDIM = 80
SCALING = HDIM ** (-0.5)
LOG2E = math.log2(math.e)
PADDED = 96
VMEM_LIMIT = 24 * 1024 * 1024
F32 = jnp.float32
BF16 = jnp.bfloat16


def shifted(block, axis, distance):
    devices = range(lax.axis_size(axis))
    route = [((i - distance) % len(devices), i) for i in devices]
    return lax.ppermute(block, axis, route)


def tile_terms(query_h, cotan_h, lse_rows, delta_rows, key_h, value_h):
    query_rows = query_h.shape[0]
    key_rows = key_h.shape[0]
    groups = query_h.shape[1]
    scores = (
        jnp.einsum("qhd,khd->hqk", query_h, key_h, preferred_element_type=jnp.float32) * SCALING
    )
    probs = jnp.exp(scores - lse_rows[:, :, None])
    probs16 = probs.astype(jnp.bfloat16)
    value_part = jnp.einsum("hqk,qhd->khd", probs16, cotan_h, preferred_element_type=jnp.float32)
    dprobs = jnp.einsum("qhd,khd->hqk", cotan_h, value_h, preferred_element_type=jnp.float32)
    dscores = (probs * (dprobs - delta_rows[:, :, None])).astype(jnp.bfloat16)
    query_part = jnp.einsum("hqk,khd->qhd", dscores, key_h, preferred_element_type=jnp.float32)
    key_part = jnp.einsum("hqk,qhd->khd", dscores, query_h, preferred_element_type=jnp.float32)
    return (
        query_part.reshape(query_rows, groups * HDIM),
        key_part.reshape(key_rows, groups * HDIM),
        value_part.reshape(key_rows, groups * HDIM),
    )


def crop_terms(query_h, cotan_h, lse_rows, delta_rows, key_h, value_h):
    return lax.map(
        lambda pieces: tile_terms(*pieces), (query_h, cotan_h, lse_rows, delta_rows, key_h, value_h)
    )


def ring_body(queries, keys, values, outputs, grad_out, lse):
    crops = queries.shape[0]
    groups = lse.shape[1]
    rows = lse.shape[2]
    query_own, key_own, value_own, cotan_own, output_own = (
        lax.all_to_all(sent, "head", split_axis=2, concat_axis=1, tiled=True)
        for sent in (queries, keys, values, grad_out, outputs)
    )
    products = cotan_own.astype(jnp.float32) * output_own.astype(jnp.float32)
    delta_rows = jnp.transpose(
        jnp.sum(products.reshape(crops, rows, groups, HDIM), axis=-1), (0, 2, 1)
    )
    query_h = query_own.reshape(crops, rows, groups, HDIM)
    cotan_h = cotan_own.reshape(crops, rows, groups, HDIM)
    key_h = key_own.reshape(crops, rows, groups, HDIM)
    value_h = value_own.reshape(crops, rows, groups, HDIM)
    width = groups * HDIM
    nblocks = lax.axis_size("blk")
    zeros_acc = jnp.zeros((crops, rows, width), jnp.float32)
    start = (query_h, cotan_h, lse, delta_rows, zeros_acc, zeros_acc, zeros_acc)

    def cycle_step(index, carry):
        query_cur, cotan_cur, lse_cur, delta_cur, query_acc, key_acc, value_acc = carry
        query_part, key_part, value_part = crop_terms(
            query_cur, cotan_cur, lse_cur, delta_cur, key_h, value_h
        )
        query_acc, lse_cur, delta_cur = shifted(
            (query_acc + query_part, lse_cur, delta_cur), "blk", 1
        )
        query_cur, cotan_cur = shifted((query_cur, cotan_cur), "blk", 1)
        return (
            query_cur,
            cotan_cur,
            lse_cur,
            delta_cur,
            query_acc,
            key_acc + key_part,
            value_acc + value_part,
        )

    query_cur, cotan_cur, lse_cur, delta_cur, query_acc, key_acc, value_acc = lax.fori_loop(
        0, nblocks - 1, cycle_step, start
    )
    query_part, key_part, value_part = crop_terms(
        query_cur, cotan_cur, lse_cur, delta_cur, key_h, value_h
    )
    query_total = shifted((query_acc + query_part).astype(jnp.bfloat16), "blk", 1).astype(
        jnp.float32
    )
    grad_q16 = (query_total * SCALING).astype(jnp.bfloat16)
    grad_k16 = ((key_acc + key_part) * SCALING).astype(jnp.bfloat16)
    grad_v16 = (value_acc + value_part).astype(jnp.bfloat16)
    return tuple(
        lax.all_to_all(grad, "head", split_axis=1, concat_axis=2, tiled=True)
        for grad in (grad_q16, grad_k16, grad_v16)
    )


def call(kernel, out_shape, *operands, scratch=(), remote=0, out_space=pltpu.VMEM, limit=VMEM_LIMIT):
    specs = [
        pl.BlockSpec(memory_space=pltpu.HBM if i < remote else pltpu.VMEM)
        for i in range(len(operands))
    ]
    return pl.pallas_call(
        kernel,
        out_shape=out_shape,
        in_specs=specs,
        out_specs=jax.tree.map(lambda _: pl.BlockSpec(memory_space=out_space), out_shape),
        scratch_shapes=list(scratch),
        compiler_params=pltpu.CompilerParams(vmem_limit_bytes=limit),
    )(*operands)


def place():
    h, b = lax.axis_index("head"), lax.axis_index("blk")
    return lax.div(h, 2), lax.rem(lax.div(b, 2), 2), lax.rem(h, 2), h


def shape(*dims, dtype=BF16):
    return jax.ShapeDtypeStruct(dims, dtype)


def head_of(array, head):
    return array[:, HDIM * head : HDIM * (head + 1)]


def pieces_of(row):
    high = row.astype(BF16)
    rest = row - high.astype(F32)
    middle = rest.astype(BF16)
    low = (rest - middle.astype(F32)).astype(BF16)
    return jnp.concatenate([high.astype(F32), middle.astype(F32), low.astype(F32)], axis=0)


def pack_inputs_kernel(
    q_in, k_in, v_in, o_in, do_in, lse_in, out0, out1, out2, out3,
    q_s, k_s, v_s, o_s, do_s, lse_s, out_ref, done, sent,
):
    x, w, c, _ = place()
    copies = [
        pltpu.make_async_copy(source, target, done.at[i])
        for i, (source, target) in enumerate(
            ((q_in, q_s), (k_in, k_s), (v_in, v_s), (do_in, do_s), (o_in, o_s), (lse_in, lse_s))
        )
    ]
    for copy in copies:
        copy.start()
    for copy in copies:
        copy.wait()
    rows = q_s.shape[0]
    q, k, v, do = q_s[...], k_s[...], v_s[...], do_s[...]
    outs = (out0, out1, out2, out3)

    def leave(part, spot):
        return [
            pltpu.make_async_copy(out_ref.at[j, spot], out.at[spot], sent.at[4 * part + j])
            for j, out in enumerate(outs)
        ]

    for side in range(2):

        @pl.when(c == side)
        def _():
            for xs in range(2):
                for ws in range(2):
                    near, deep = [], []
                    for cs in (side, 1 - side):
                        head = 4 * xs + 2 * cs + ws
                        value = head_of(v, head)
                        near += [head_of(q, head), head_of(do, head), head_of(k, head), value[:, :16]]
                        deep.append(value[:, 16:])
                    j = 2 * (x ^ xs) + (w ^ ws)
                    out_ref[j, 0:rows] = jnp.concatenate(near + deep, axis=1)

    most = leave(0, pl.ds(0, PADDED - 16))
    for copy in most:
        copy.start()
    products = do.astype(F32) * o_s[...].astype(F32)
    high = products.astype(BF16)
    rest = products - high.astype(F32)
    middle = rest.astype(BF16)
    low = (rest - middle.astype(F32)).astype(BF16)
    row = lax.broadcasted_iota(jnp.int32, (8, 640), 0)
    lane = lax.broadcasted_iota(jnp.int32, (8, 640), 1)
    mine = jnp.where((lane >= HDIM * row) & (lane < HDIM * (row + 1)), 1.0, 0.0).astype(BF16)
    deltas = sum(
        lax.dot_general(mine, part, (((1,), (1,)), ((), ())), preferred_element_type=F32)
        for part in (low, middle, high)
    )
    lse = lse_s[pl.ds(1 - w, 1), :] * LOG2E
    lse = jnp.concatenate([lse[:, rows * i : rows * (i + 1)] for i in range(4)], axis=0)
    lse = pieces_of(lse)
    blank = jnp.zeros((3, 128 - rows), F32)
    gap = jnp.zeros((5, 128), F32)
    edge = jnp.zeros((8, 128 - rows), F32)
    sides = [
        jnp.concatenate([lse[0:8], edge], axis=1),
        jnp.concatenate([jnp.concatenate([lse[8:12], lse[8:12]], axis=0), edge], axis=1),
    ]
    for xs in range(2):
        for ws in range(2):
            j = 2 * (x ^ xs) + (w ^ ws)
            pair = []
            for cs in range(2):
                head = 4 * xs + 2 * cs + ws
                delta = jnp.concatenate([pieces_of(deltas[head : head + 1, :]), blank], axis=1)
                pair.append(jnp.concatenate([delta, gap], axis=0))
            kept = jnp.where(c == 0, pair[0], pair[1])
            given = jnp.where(c == 0, pair[1], pair[0])
            spots = [kept, sides[0], given, sides[1], jnp.zeros((8, 128), F32)]
            out_ref[j, rows:PADDED] = jnp.concatenate(spots, axis=1).astype(BF16)
    last = leave(1, pl.ds(PADDED - 16, 16))
    for copy in last:
        copy.start()
    for copy in most + last:
        copy.wait()


def gather_kernel(first, block_a, block_b, other_a, other_b, near1, lse_in, queries, keys, lse_s):
    rows = keys.shape[0]
    _, w, _, h = place()
    lse_own = lse_in[pl.ds(w, 1), :] * LOG2E
    below = near1[rows:PADDED, :].astype(F32)
    lse_near = below[0:4, 128 : 128 + rows] + below[4:8, 128 : 128 + rows]
    lse_near = lse_near + below[0:4, 384 : 384 + rows]
    lse_s[...] = jnp.concatenate(
        [lse_own[:, rows * i : rows * (i + 1)] for i in range(4)] + [lse_near], axis=0
    )
    q_parts, k_parts, spots = [], [], []
    gap = jnp.zeros((6, PADDED - rows), F32)
    for j in (first, first + 1):
        for r in range(2):
            held = ((block_a, block_b), (other_a, other_b))[r][j % 2]
            deep = (512, 320)[r]
            q_parts.append(held[0:rows, 0:160])
            k_parts += [held[0:rows, 160:256], held[0:rows, deep : deep + 64]]
            delta = held[rows:PADDED, 0:128].astype(F32)[0:3, 0:rows]
            lse = lse_s[pl.ds(4 * (j % 2) + (h ^ (2 * (j // 2) + r)), 1), :]
            spots += [jnp.concatenate([delta, pieces_of(lse)], axis=0), gap]
    keys[...] = jnp.concatenate(k_parts, axis=1)
    queries[0:rows] = jnp.concatenate(q_parts, axis=1)
    below = jnp.concatenate(spots + [jnp.zeros((6, 256), F32)], axis=1)
    below = jnp.concatenate([below, jnp.zeros((2, 640), F32)], axis=0)
    queries[rows:PADDED] = below.astype(BF16)


def rows_of(wires):
    rows = PADDED - 8
    below = jnp.concatenate(
        [wire[rows:PADDED, 0 : 4 * PADDED].astype(F32) for wire in wires], axis=1
    )
    return below[3:4] + below[4:5] + below[5:6], below[0:1] + below[1:2] + below[2:3]


def spread(wide, left, right, first=0):
    rows = PADDED - 8
    blank = jnp.zeros((16, HDIM), BF16)
    for i in range(wide.shape[1] // (2 * HDIM)):
        at, lane = PADDED * (first + i), 2 * HDIM * i
        for target, start in ((left, lane), (right, lane + HDIM)):
            target[pl.ds(at + PADDED - 16, 16), :] = blank
            target[pl.ds(at, rows), :] = wide[0:rows, start : start + HDIM]


def tile_step(q, do, k_s, v_s, lse, delta, chunk=384):
    q_t, do_t = q.T, do.T
    k_t = k_s[...].T
    dq_t = None
    parts = []
    for start in range(0, k_s.shape[0], chunk):
        spot = slice(start, start + chunk)
        k, v = k_s[spot, :], v_s[spot, :]
        scores = jnp.dot(k, q_t, preferred_element_type=F32)
        probs = jnp.exp2(scores * (SCALING * LOG2E) - lse)
        dv = jnp.dot(probs.astype(BF16), do, preferred_element_type=F32)
        dprobs = jnp.dot(v, do_t, preferred_element_type=F32)
        dscores = (probs * (dprobs - delta)).astype(BF16)
        dk = jnp.dot(dscores, q, preferred_element_type=F32)
        more = jnp.dot(k_t[:, spot], dscores, preferred_element_type=F32)
        dq_t = more if dq_t is None else dq_t + more
        parts.append((spot, dk, dv))
    return dq_t, parts


def to_wire(arrays, rows):
    count = arrays[0].shape[0] // PADDED
    return jnp.concatenate(
        [a[PADDED * i : PADDED * i + rows].astype(BF16) for i in range(count) for a in arrays],
        axis=1,
    )


def own_own_kernel(low, high, k_low, k_high, dq_t, dk, dv, q_s, do_s, k_s, v_s):
    spread(low, q_s, do_s)
    spread(high, q_s, do_s, 4)
    spread(k_low, k_s, v_s)
    spread(k_high, k_s, v_s, 4)
    dq_t[...], parts = tile_step(q_s[...], do_s[...], k_s, v_s, *rows_of([low, high]))
    for spot, dk_part, dv_part in parts:
        dk[spot, :] = dk_part
        dv[spot, :] = dv_part


def own_far_kernel(low, high, q_s, do_s, k_low, k_high, dq_before, dq_t, dk, dv, k_s, v_s):
    spread(k_low, k_s, v_s)
    spread(k_high, k_s, v_s, 4)
    more, parts = tile_step(q_s[...], do_s[...], k_s, v_s, *rows_of([low, high]))
    dq_t[...] = dq_before[...] + more
    for spot, dk_part, dv_part in parts:
        dk[spot, :] = dk_part
        dv[spot, :] = dv_part


def low_kernel(
    low, k_far, v_far, k_own, v_own, dk_far_in, dv_far_in, dk_own_in, dv_own_in,
    dq_t, dk_far, dv_far, dk_own, dv_own, q_s, do_s,
):
    spread(low, q_s, do_s)
    q, do = q_s[...], do_s[...]
    lse, delta = rows_of([low])
    total = None
    for k_s, v_s, dk_in, dv_in, dk, dv in (
        (k_far, v_far, dk_far_in, dv_far_in, dk_far, dv_far),
        (k_own, v_own, dk_own_in, dv_own_in, dk_own, dv_own),
    ):
        more, parts = tile_step(q, do, k_s, v_s, lse, delta)
        total = more if total is None else total + more
        for spot, dk_part, dv_part in parts:
            dk[spot, :] = dk_in[spot, :] + dk_part
            dv[spot, :] = dv_in[spot, :] + dv_part
    dq_t[...] = total


def high_far_kernel(high, k_far, v_far, dk_in, dv_in, dq_t, wire, q_s, do_s, dk, dv):
    spread(high, q_s, do_s)
    dq_t[...], parts = tile_step(q_s[...], do_s[...], k_far, v_far, *rows_of([high]))
    for spot, dk_part, dv_part in parts:
        dk[spot, :] = (dk_in[spot, :] + dk_part) * SCALING
        dv[spot, :] = dv_in[spot, :] + dv_part
    wire[...] = to_wire([dk[...], dv[...]], wire.shape[0])


def high_own_kernel(
    high, q_s, do_s, k_own, v_own, dq_low, dq_high, dk_in, dv_in, wire, dk, dv
):
    more, parts = tile_step(q_s[...], do_s[...], k_own, v_own, *rows_of([high]))
    dq = jnp.concatenate([dq_low[...], dq_high[...] + more], axis=1) * SCALING
    wire[...] = to_wire([dq.T], wire.shape[0])
    for spot, dk_part, dv_part in parts:
        dk[spot, :] = dk_in[spot, :] + dk_part
        dv[spot, :] = dv_in[spot, :] + dv_part


def own_grads_kernel(dq_t, dk, dv, out):
    rows = out.shape[1]
    dq = dq_t[...].T * SCALING
    zeros = jnp.zeros((rows, 16), F32)
    for i in range(8):
        spot = slice(PADDED * i, PADDED * i + rows)
        block = jnp.concatenate([dq[spot], dk[spot, :] * SCALING, dv[spot, :], zeros], axis=1)
        out[i // 2, :, 256 * (i % 2) : 256 * (i % 2) + 256] = block


def pack_grads_kernel(own, dkv_wire, dq_wire, out):
    rows = dkv_wire.shape[0]
    dq = dq_wire[...]
    dkv = dkv_wire[...]
    zeros = jnp.zeros((rows, 16), BF16)
    for i in range(8):
        block = jnp.concatenate(
            [
                dq[:, HDIM * i : HDIM * (i + 1)],
                dkv[:, 2 * HDIM * i : 2 * HDIM * (i + 1)],
                zeros,
            ],
            axis=1,
        )
        lanes = slice(256 * (i % 2), 256 * (i % 2) + 256)
        out[i // 2, :, lanes] = (own[i // 2, :, lanes] + block.astype(F32)).astype(BF16)


def unpack_grads_kernel(*refs):
    kept, given, dq, dk, dv, held, other = refs[0:4], refs[4:8], *refs[8:]
    x, w, c, _ = place()
    for j in range(4):
        held[j] = kept[j][:, 0:256]
        other[j] = given[j][...]
    blocks = []
    for head in range(8):
        xs, cs, ws = head // 4, (head // 2) % 2, head % 2
        j = 2 * (x ^ xs) + (w ^ ws)
        blocks.append(jnp.where(c == cs, held[j].astype(F32), other[j].astype(F32)).astype(BF16))
    for k, out in enumerate((dq, dk, dv)):
        out[...] = jnp.concatenate(
            [block[:, HDIM * k : HDIM * (k + 1)] for block in blocks], axis=1
        )


def flipped(array, head_bits, blk_bits):
    heads, blks = lax.axis_size("head"), lax.axis_size("blk")
    if not blk_bits:
        return lax.ppermute(array, "head", [(i, i ^ head_bits) for i in range(heads)])
    if not head_bits:
        return lax.ppermute(array, "blk", [(i, i ^ blk_bits) for i in range(blks)])
    bits = head_bits * blks + blk_bits
    return lax.ppermute(array, ("head", "blk"), [(i, i ^ bits) for i in range(heads * blks)])


def to_chips(packed):
    return [flipped(packed[1], 0, 2), flipped(packed[2], 2, 0), flipped(packed[3], 2, 2)]


def grid_body(queries, keys, values, outputs, grad_out, lse):
    rows = queries.shape[1]
    padded = 8 * PADDED
    half = padded // 2

    packed = call(
        pack_inputs_kernel,
        (shape(PADDED, 640),) * 4,
        queries[0], keys[0], values[0], outputs[0], grad_out[0], lse[0],
        remote=6,
        out_space=pltpu.HBM,
        limit=57 * 1024 * 1024,
        scratch=[pltpu.VMEM(queries.shape[1:], BF16)] * 5
        + [pltpu.VMEM(lse.shape[1:], F32), pltpu.VMEM((4, PADDED, 640), BF16)]
        + [pltpu.SemaphoreType.DMA((6,)), pltpu.SemaphoreType.DMA((8,))],
    )
    own = packed[0]
    near = to_chips(packed)
    other = [flipped(a[:, 256:], 1, 0) for a in [own] + near]
    blocks = [own] + near

    def gather(first):
        return call(
            functools.partial(gather_kernel, first),
            (shape(PADDED, 640), shape(rows, 640)),
            *blocks[first : first + 2], *other[first : first + 2], near[0], lse[0],
            scratch=[pltpu.VMEM((8, rows), F32)],
        )

    low, k_low = gather(0)
    low_far, k_low_far = flipped(low, 0, 4), flipped(k_low, 0, 1)
    high, k_high = gather(2)
    k_high, k_low_far = lax.optimization_barrier((k_high, k_low_far))
    high_far, k_high_far = flipped(high, 0, 4), flipped(k_high, 0, 1)
    keys_far = [k_low_far, k_high_far]

    grad = shape(padded, HDIM, dtype=F32)
    side = shape(padded, HDIM)
    dq_shape = shape(HDIM, padded, dtype=F32)
    dq_own, dk_own, dv_own, q_s, do_s, k_own, v_own = call(
        own_own_kernel, (dq_shape, grad, grad, side, side, side, side), low, high, k_low, k_high
    )
    dq_own, dk_far, dv_far, k_far, v_far = call(
        own_far_kernel, (dq_shape, grad, grad, side, side), low, high, q_s, do_s, *keys_far, dq_own
    )
    dq_low, dk_far, dv_far, dk_own, dv_own = call(
        low_kernel, (shape(HDIM, half, dtype=F32), grad, grad, grad, grad),
        low_far, k_far, v_far, k_own, v_own, dk_far, dv_far, dk_own, dv_own,
        scratch=[pltpu.VMEM((half, HDIM), BF16)] * 2,
    )
    few = shape(half, HDIM)
    dq_high, dkv_wire, q_s, do_s = call(
        high_far_kernel,
        (shape(HDIM, half, dtype=F32), shape(rows, 1280), few, few),
        high_far, k_far, v_far, dk_far, dv_far,
        scratch=[pltpu.VMEM((padded, HDIM), F32)] * 2,
    )
    dkv_back = flipped(dkv_wire, 0, 1)
    dq_wire, dk_own, dv_own = call(
        high_own_kernel, (shape(rows, 640), grad, grad),
        high_far, q_s, do_s, k_own, v_own, dq_low, dq_high, dk_own, dv_own,
    )
    dq_back = flipped(dq_wire, 0, 4)
    own_g = call(own_grads_kernel, shape(4, rows, 512, dtype=F32), dq_own, dk_own, dv_own)
    packed_g = call(pack_grads_kernel, shape(4, rows, 512), own_g, dkv_back, dq_back)
    held = [packed_g[0]] + to_chips(packed_g)
    other = [flipped(a[:, 256:], 1, 0) for a in held]
    out = shape(rows, queries.shape[2])
    grads = call(
        unpack_grads_kernel, (out, out, out), *held, *other,
        scratch=[pltpu.VMEM((4, rows, 256), BF16)] * 2,
    )
    return tuple(grad[None] for grad in grads)


def solution(mesh):
    placed = P(None, ("blk", "head"), None)
    on_grid = mesh.shape["head"] == 4 and mesh.shape["blk"] == 8
    return jax.shard_map(
        grid_body if on_grid else ring_body,
        mesh=mesh,
        in_specs=(placed,) * 5 + (P(None, "head", "blk"),),
        out_specs=(placed,) * 3,
        check_vma=False,
    )
```

```python
import functools
import math

import jax
import jax.numpy as jnp
from jax import lax
from jax.experimental import pallas as pl
from jax.experimental.pallas import tpu as pltpu
from jax.sharding import PartitionSpec as P

HDIM = 80
SCALING = HDIM ** (-0.5)
LOG2E = math.log2(math.e)
PADDED = 96
LOW = 3
LOW_KEYS = 3
VMEM_LIMIT = 24 * 1024 * 1024
F32 = jnp.float32
BF16 = jnp.bfloat16


def shifted(block, axis, distance):
    devices = range(lax.axis_size(axis))
    route = [((i - distance) % len(devices), i) for i in devices]
    return lax.ppermute(block, axis, route)


def tile_terms(query_h, cotan_h, lse_rows, delta_rows, key_h, value_h):
    query_rows = query_h.shape[0]
    key_rows = key_h.shape[0]
    groups = query_h.shape[1]
    scores = (
        jnp.einsum("qhd,khd->hqk", query_h, key_h, preferred_element_type=jnp.float32) * SCALING
    )
    probs = jnp.exp(scores - lse_rows[:, :, None])
    probs16 = probs.astype(jnp.bfloat16)
    value_part = jnp.einsum("hqk,qhd->khd", probs16, cotan_h, preferred_element_type=jnp.float32)
    dprobs = jnp.einsum("qhd,khd->hqk", cotan_h, value_h, preferred_element_type=jnp.float32)
    dscores = (probs * (dprobs - delta_rows[:, :, None])).astype(jnp.bfloat16)
    query_part = jnp.einsum("hqk,khd->qhd", dscores, key_h, preferred_element_type=jnp.float32)
    key_part = jnp.einsum("hqk,qhd->khd", dscores, query_h, preferred_element_type=jnp.float32)
    return (
        query_part.reshape(query_rows, groups * HDIM),
        key_part.reshape(key_rows, groups * HDIM),
        value_part.reshape(key_rows, groups * HDIM),
    )


def crop_terms(query_h, cotan_h, lse_rows, delta_rows, key_h, value_h):
    return lax.map(
        lambda pieces: tile_terms(*pieces), (query_h, cotan_h, lse_rows, delta_rows, key_h, value_h)
    )


def ring_body(queries, keys, values, outputs, grad_out, lse):
    crops = queries.shape[0]
    groups = lse.shape[1]
    rows = lse.shape[2]
    query_own, key_own, value_own, cotan_own, output_own = (
        lax.all_to_all(sent, "head", split_axis=2, concat_axis=1, tiled=True)
        for sent in (queries, keys, values, grad_out, outputs)
    )
    products = cotan_own.astype(jnp.float32) * output_own.astype(jnp.float32)
    delta_rows = jnp.transpose(
        jnp.sum(products.reshape(crops, rows, groups, HDIM), axis=-1), (0, 2, 1)
    )
    query_h = query_own.reshape(crops, rows, groups, HDIM)
    cotan_h = cotan_own.reshape(crops, rows, groups, HDIM)
    key_h = key_own.reshape(crops, rows, groups, HDIM)
    value_h = value_own.reshape(crops, rows, groups, HDIM)
    width = groups * HDIM
    nblocks = lax.axis_size("blk")
    zeros_acc = jnp.zeros((crops, rows, width), jnp.float32)
    start = (query_h, cotan_h, lse, delta_rows, zeros_acc, zeros_acc, zeros_acc)

    def cycle_step(index, carry):
        query_cur, cotan_cur, lse_cur, delta_cur, query_acc, key_acc, value_acc = carry
        query_part, key_part, value_part = crop_terms(
            query_cur, cotan_cur, lse_cur, delta_cur, key_h, value_h
        )
        query_acc, lse_cur, delta_cur = shifted(
            (query_acc + query_part, lse_cur, delta_cur), "blk", 1
        )
        query_cur, cotan_cur = shifted((query_cur, cotan_cur), "blk", 1)
        return (
            query_cur,
            cotan_cur,
            lse_cur,
            delta_cur,
            query_acc,
            key_acc + key_part,
            value_acc + value_part,
        )

    query_cur, cotan_cur, lse_cur, delta_cur, query_acc, key_acc, value_acc = lax.fori_loop(
        0, nblocks - 1, cycle_step, start
    )
    query_part, key_part, value_part = crop_terms(
        query_cur, cotan_cur, lse_cur, delta_cur, key_h, value_h
    )
    query_total = shifted((query_acc + query_part).astype(jnp.bfloat16), "blk", 1).astype(
        jnp.float32
    )
    grad_q16 = (query_total * SCALING).astype(jnp.bfloat16)
    grad_k16 = ((key_acc + key_part) * SCALING).astype(jnp.bfloat16)
    grad_v16 = (value_acc + value_part).astype(jnp.bfloat16)
    return tuple(
        lax.all_to_all(grad, "head", split_axis=1, concat_axis=2, tiled=True)
        for grad in (grad_q16, grad_k16, grad_v16)
    )


def call(kernel, out_shape, *operands, scratch=(), remote=0, out_space=pltpu.VMEM, limit=VMEM_LIMIT):
    specs = [
        pl.BlockSpec(memory_space=pltpu.HBM if i < remote else pltpu.VMEM)
        for i in range(len(operands))
    ]
    return pl.pallas_call(
        kernel,
        out_shape=out_shape,
        in_specs=specs,
        out_specs=jax.tree.map(lambda _: pl.BlockSpec(memory_space=out_space), out_shape),
        scratch_shapes=list(scratch),
        compiler_params=pltpu.CompilerParams(vmem_limit_bytes=limit),
    )(*operands)


def place():
    h, b = lax.axis_index("head"), lax.axis_index("blk")
    return lax.div(h, 2), lax.rem(lax.div(b, 2), 2), lax.rem(h, 2), h


def shape(*dims, dtype=BF16):
    return jax.ShapeDtypeStruct(dims, dtype)


def head_of(array, head):
    return array[:, HDIM * head : HDIM * (head + 1)]


def pieces_of(row):
    high = row.astype(BF16)
    rest = row - high.astype(F32)
    middle = rest.astype(BF16)
    low = (rest - middle.astype(F32)).astype(BF16)
    return jnp.concatenate([high.astype(F32), middle.astype(F32), low.astype(F32)], axis=0)


def pack_inputs_kernel(
    q_in, k_in, v_in, o_in, do_in, lse_in, out0, out1, out2, out3,
    q_s, k_s, v_s, o_s, do_s, lse_s, out_ref, done, sent,
):
    x, w, c, _ = place()
    copies = [
        pltpu.make_async_copy(source, target, done.at[i])
        for i, (source, target) in enumerate(
            ((q_in, q_s), (k_in, k_s), (v_in, v_s), (do_in, do_s), (o_in, o_s), (lse_in, lse_s))
        )
    ]
    for copy in copies:
        copy.start()
    for copy in copies:
        copy.wait()
    rows = q_s.shape[0]
    q, k, v, do = q_s[...], k_s[...], v_s[...], do_s[...]
    outs = (out0, out1, out2, out3)

    def leave(part, spot):
        return [
            pltpu.make_async_copy(out_ref.at[j, spot], out.at[spot], sent.at[4 * part + j])
            for j, out in enumerate(outs)
        ]

    for side in range(2):

        @pl.when(c == side)
        def _():
            for xs in range(2):
                for ws in range(2):
                    near, deep = [], []
                    for cs in (side, 1 - side):
                        head = 4 * xs + 2 * cs + ws
                        value = head_of(v, head)
                        near += [head_of(q, head), head_of(do, head), head_of(k, head), value[:, :16]]
                        deep.append(value[:, 16:])
                    j = 2 * (x ^ xs) + (w ^ ws)
                    out_ref[j, 0:rows] = jnp.concatenate(near + deep, axis=1)

    most = leave(0, pl.ds(0, PADDED - 16))
    for copy in most:
        copy.start()
    products = do.astype(F32) * o_s[...].astype(F32)
    high = products.astype(BF16)
    rest = products - high.astype(F32)
    middle = rest.astype(BF16)
    low = (rest - middle.astype(F32)).astype(BF16)
    row = lax.broadcasted_iota(jnp.int32, (8, 640), 0)
    lane = lax.broadcasted_iota(jnp.int32, (8, 640), 1)
    mine = jnp.where((lane >= HDIM * row) & (lane < HDIM * (row + 1)), 1.0, 0.0).astype(BF16)
    deltas = sum(
        lax.dot_general(mine, part, (((1,), (1,)), ((), ())), preferred_element_type=F32)
        for part in (low, middle, high)
    )
    lse = lse_s[pl.ds(1 - w, 1), :] * LOG2E
    lse = jnp.concatenate([lse[:, rows * i : rows * (i + 1)] for i in range(4)], axis=0)
    lse = pieces_of(lse)
    blank = jnp.zeros((3, 128 - rows), F32)
    gap = jnp.zeros((5, 128), F32)
    edge = jnp.zeros((8, 128 - rows), F32)
    sides = [
        jnp.concatenate([lse[0:8], edge], axis=1),
        jnp.concatenate([jnp.concatenate([lse[8:12], lse[8:12]], axis=0), edge], axis=1),
    ]
    for xs in range(2):
        for ws in range(2):
            j = 2 * (x ^ xs) + (w ^ ws)
            pair = []
            for cs in range(2):
                head = 4 * xs + 2 * cs + ws
                delta = jnp.concatenate([pieces_of(deltas[head : head + 1, :]), blank], axis=1)
                pair.append(jnp.concatenate([delta, gap], axis=0))
            kept = jnp.where(c == 0, pair[0], pair[1])
            given = jnp.where(c == 0, pair[1], pair[0])
            spots = [kept, sides[0], given, sides[1], jnp.zeros((8, 128), F32)]
            out_ref[j, rows:PADDED] = jnp.concatenate(spots, axis=1).astype(BF16)
    last = leave(1, pl.ds(PADDED - 16, 16))
    for copy in last:
        copy.start()
    for copy in most + last:
        copy.wait()


def gather_queries_kernel(spots, *refs):
    *parts, near1, lse_in, wire, lse_s = refs
    rows = PADDED - 8
    _, w, _, h = place()
    own = lse_in[pl.ds(w, 1), :] * LOG2E
    below = near1[rows:PADDED, :].astype(F32)
    near = below[0:4, 128 : 128 + rows] + below[4:8, 128 : 128 + rows]
    near = near + below[0:4, 384 : 384 + rows]
    lse_s[...] = jnp.concatenate(
        [own[:, rows * i : rows * (i + 1)] for i in range(4)] + [near], axis=0
    )
    lower = []
    gap = jnp.zeros((6, PADDED - rows), F32)
    for (j, r), ref in zip(spots, parts):
        delta = ref[rows:PADDED, 0:128].astype(F32)[0:3, 0:rows]
        lse = lse_s[pl.ds(4 * (j % 2) + (h ^ (2 * (j // 2) + r)), 1), :]
        lower += [jnp.concatenate([delta, pieces_of(lse)], axis=0), gap]
    wire[0:rows] = jnp.concatenate([ref[0:rows, 0:160] for ref in parts], axis=1)
    width = wire.shape[1] - len(parts) * PADDED
    lower = jnp.concatenate(lower + [jnp.zeros((6, width), F32)], axis=1)
    lower = jnp.concatenate([lower, jnp.zeros((2, wire.shape[1]), F32)], axis=0)
    wire[rows:PADDED] = lower.astype(BF16)


def gather_keys_kernel(spots, *refs):
    *parts, keys = refs
    rows = PADDED - 8
    pieces = []
    for (_, r), ref in zip(spots, parts):
        deep = 320 if r else 512
        pieces += [ref[0:rows, 160:256], ref[0:rows, deep : deep + 64]]
    keys[0:rows] = jnp.concatenate(pieces, axis=1)
    if keys.shape[0] > rows:
        keys[rows:PADDED] = jnp.zeros((PADDED - rows, keys.shape[1]), BF16)


def rows_of(wires):
    rows = PADDED - 8
    below = jnp.concatenate(
        [
            wire[rows:PADDED, 0 : wire.shape[1] // (2 * HDIM) * PADDED].astype(F32)
            for wire in wires
        ],
        axis=1,
    )
    return below[3:4] + below[4:5] + below[5:6], below[0:1] + below[1:2] + below[2:3]


def spread(wide, left, right, first=0):
    rows = PADDED - 8
    blank = jnp.zeros((16, HDIM), BF16)
    for i in range(wide.shape[1] // (2 * HDIM)):
        at, lane = PADDED * (first + i), 2 * HDIM * i
        for target, start in ((left, lane), (right, lane + HDIM)):
            target[pl.ds(at + PADDED - 16, 16), :] = blank
            target[pl.ds(at, rows), :] = wide[0:rows, start : start + HDIM]


def tile_step(q, do, k_s, v_s, lse, delta, chunk=384):
    q_t, do_t = q.T, do.T
    k_t = k_s[...].T
    dq_t = None
    parts = []
    for start in range(0, k_s.shape[0], chunk):
        spot = slice(start, start + chunk)
        k, v = k_s[spot, :], v_s[spot, :]
        scores = jnp.dot(k, q_t, preferred_element_type=F32)
        probs = jnp.exp2(scores * (SCALING * LOG2E) - lse)
        dv = jnp.dot(probs.astype(BF16), do, preferred_element_type=F32)
        dprobs = jnp.dot(v, do_t, preferred_element_type=F32)
        dscores = (probs * (dprobs - delta)).astype(BF16)
        dk = jnp.dot(dscores, q, preferred_element_type=F32)
        more = jnp.dot(k_t[:, spot], dscores, preferred_element_type=F32)
        dq_t = more if dq_t is None else dq_t + more
        parts.append((spot, dk, dv))
    return dq_t, parts


def to_wire(arrays, rows):
    count = arrays[0].shape[0] // PADDED
    return jnp.concatenate(
        [a[PADDED * i : PADDED * i + rows].astype(BF16) for i in range(count) for a in arrays],
        axis=1,
    )


def own_own_kernel(low, high, k_low, k_high, dq_t, dk, dv, q_s, do_s, k_s, v_s):
    spread(low, q_s, do_s)
    spread(high, q_s, do_s, LOW)
    spread(k_low, k_s, v_s)
    spread(k_high, k_s, v_s, LOW_KEYS)
    dq_t[...], parts = tile_step(q_s[...], do_s[...], k_s, v_s, *rows_of([low, high]))
    for spot, dk_part, dv_part in parts:
        dk[spot, :] = dk_part
        dv[spot, :] = dv_part


def own_far_kernel(after, low, high, q_s, do_s, k_low, k_high, dq_before, dq_t, dk, dv, k_s, v_s):
    spread(k_low, k_s, v_s)
    spread(k_high, k_s, v_s, LOW_KEYS)
    more, parts = tile_step(q_s[...], do_s[...], k_s, v_s, *rows_of([low, high]))
    dq_t[...] = dq_before[...] + more
    for spot, dk_part, dv_part in parts:
        dk[spot, :] = dk_part
        dv[spot, :] = dv_part


def low_own_kernel(wire, k_own, v_own, dk_in, dv_in, dq_t, dk, dv, q_s, do_s):
    spread(wire, q_s, do_s)
    dq_t[...], parts = tile_step(q_s[...], do_s[...], k_own, v_own, *rows_of([wire]))
    for spot, dk_part, dv_part in parts:
        dk[spot, :] = dk_in[spot, :] + dk_part
        dv[spot, :] = dv_in[spot, :] + dv_part


def low_far_kernel(wire, q_s, do_s, k_far, v_far, dq_before, dk_in, dv_in, dq_t, dk, dv):
    more, parts = tile_step(q_s[...], do_s[...], k_far, v_far, *rows_of([wire]))
    dq_t[...] = dq_before[...] + more
    for spot, dk_part, dv_part in parts:
        dk[spot, :] = dk_in[spot, :] + dk_part
        dv[spot, :] = dv_in[spot, :] + dv_part


def high_far_kernel(high, k_far, v_far, dk_in, dv_in, dq_t, wire, q_s, do_s, dk, dv):
    spread(high, q_s, do_s)
    dq_t[...], parts = tile_step(q_s[...], do_s[...], k_far, v_far, *rows_of([high]))
    for spot, dk_part, dv_part in parts:
        dk[spot, :] = (dk_in[spot, :] + dk_part) * SCALING
        dv[spot, :] = dv_in[spot, :] + dv_part
    wire[...] = to_wire([dk[...], dv[...]], wire.shape[0])


def high_own_kernel(
    high, q_s, do_s, k_own, v_own, dq_low, dq_high, dk_in, dv_in, wire, dk, dv
):
    more, parts = tile_step(q_s[...], do_s[...], k_own, v_own, *rows_of([high]))
    dq = jnp.concatenate([dq_low[...], dq_high[...] + more], axis=1) * SCALING
    wire[...] = to_wire([dq.T], wire.shape[0])
    for spot, dk_part, dv_part in parts:
        dk[spot, :] = dk_in[spot, :] + dk_part
        dv[spot, :] = dv_in[spot, :] + dv_part


def own_grads_kernel(dq_t, dk, dv, out):
    rows = out.shape[1]
    dq = dq_t[...].T * SCALING
    zeros = jnp.zeros((rows, 16), F32)
    for i in range(8):
        spot = slice(PADDED * i, PADDED * i + rows)
        block = jnp.concatenate([dq[spot], dk[spot, :] * SCALING, dv[spot, :], zeros], axis=1)
        out[i // 2, :, 256 * (i % 2) : 256 * (i % 2) + 256] = block


def pack_grads_kernel(own, dkv_wire, dq_wire, out):
    rows = dkv_wire.shape[0]
    dq = dq_wire[...]
    dkv = dkv_wire[...]
    zeros = jnp.zeros((rows, 16), BF16)
    for i in range(8):
        block = jnp.concatenate(
            [
                dq[:, HDIM * i : HDIM * (i + 1)],
                dkv[:, 2 * HDIM * i : 2 * HDIM * (i + 1)],
                zeros,
            ],
            axis=1,
        )
        lanes = slice(256 * (i % 2), 256 * (i % 2) + 256)
        out[i // 2, :, lanes] = (own[i // 2, :, lanes] + block.astype(F32)).astype(BF16)


def unpack_grads_kernel(*refs):
    kept, given, dq, dk, dv, held, other = refs[0:4], refs[4:8], *refs[8:]
    x, w, c, _ = place()
    for j in range(4):
        held[j] = kept[j][:, 0:256]
        other[j] = given[j][...]
    blocks = []
    for head in range(8):
        xs, cs, ws = head // 4, (head // 2) % 2, head % 2
        j = 2 * (x ^ xs) + (w ^ ws)
        blocks.append(jnp.where(c == cs, held[j].astype(F32), other[j].astype(F32)).astype(BF16))
    for k, out in enumerate((dq, dk, dv)):
        out[...] = jnp.concatenate(
            [block[:, HDIM * k : HDIM * (k + 1)] for block in blocks], axis=1
        )


def flipped(array, head_bits, blk_bits):
    heads, blks = lax.axis_size("head"), lax.axis_size("blk")
    if not blk_bits:
        return lax.ppermute(array, "head", [(i, i ^ head_bits) for i in range(heads)])
    if not head_bits:
        return lax.ppermute(array, "blk", [(i, i ^ blk_bits) for i in range(blks)])
    bits = head_bits * blks + blk_bits
    return lax.ppermute(array, ("head", "blk"), [(i, i ^ bits) for i in range(heads * blks)])


def to_chips(packed):
    return [flipped(packed[1], 0, 2), flipped(packed[2], 2, 0), flipped(packed[3], 2, 2)]


def grid_body(queries, keys, values, outputs, grad_out, lse):
    rows = queries.shape[1]
    padded = 8 * PADDED
    few = LOW * PADDED

    packed = call(
        pack_inputs_kernel,
        (shape(PADDED, 640),) * 4,
        queries[0], keys[0], values[0], outputs[0], grad_out[0], lse[0],
        remote=6,
        out_space=pltpu.HBM,
        limit=57 * 1024 * 1024,
        scratch=[pltpu.VMEM(queries.shape[1:], BF16)] * 5
        + [pltpu.VMEM(lse.shape[1:], F32), pltpu.VMEM((4, PADDED, 640), BF16)]
        + [pltpu.SemaphoreType.DMA((6,)), pltpu.SemaphoreType.DMA((8,))],
    )
    own = packed[0]
    near = to_chips(packed)
    other = [flipped(a[:, 256:], 1, 0) for a in [own] + near]
    blocks = [ref for pair in zip([own] + near, other) for ref in pair]
    spots = [(j, r) for j in range(4) for r in range(2)]

    def gather_queries(first, last):
        return call(
            functools.partial(gather_queries_kernel, spots[first:last]),
            shape(PADDED, 160 * (last - first)),
            *blocks[first:last], near[0], lse[0],
            scratch=[pltpu.VMEM((8, rows), F32)],
        )

    def gather_keys(first, last, tall):
        return call(
            functools.partial(gather_keys_kernel, spots[first:last]),
            shape(tall, 160 * (last - first)),
            *blocks[first:last],
        )

    low, k_low = gather_queries(0, LOW), gather_keys(0, LOW_KEYS, PADDED)
    low_far, k_low_far = flipped(low, 0, 4), flipped(k_low, 0, 1)
    high, k_high = gather_queries(LOW, 8), gather_keys(LOW_KEYS, 8, rows)
    high_far = flipped(high, 0, 4)
    k_high, k_low_far, low_far = lax.optimization_barrier((k_high, k_low_far, low_far))
    k_high_far = flipped(k_high, 0, 1)
    keys_far = [k_low_far, k_high_far]

    grad = shape(padded, HDIM, dtype=F32)
    side = shape(padded, HDIM)
    dq_shape = shape(HDIM, padded, dtype=F32)
    dq_own, dk_own, dv_own, q_s, do_s, k_own, v_own = call(
        own_own_kernel, (dq_shape, grad, grad, side, side, side, side), low, high, k_low, k_high
    )
    some = shape(few, HDIM)
    dq_low, dk_own, dv_own, q_low_s, do_low_s = call(
        low_own_kernel, (shape(HDIM, few, dtype=F32), grad, grad, some, some),
        low_far, k_own, v_own, dk_own, dv_own,
    )
    dq_own, dk_far, dv_far, k_far, v_far = call(
        own_far_kernel, (dq_shape, grad, grad, side, side),
        dq_low, low, high, q_s, do_s, *keys_far, dq_own,
    )
    dq_low, dk_far, dv_far = call(
        low_far_kernel, (shape(HDIM, few, dtype=F32), grad, grad),
        low_far, q_low_s, do_low_s, k_far, v_far, dq_low, dk_far, dv_far,
    )
    most = shape(padded - few, HDIM)
    dq_high, dkv_wire, q_s, do_s = call(
        high_far_kernel,
        (shape(HDIM, padded - few, dtype=F32), shape(rows, 1280), most, most),
        high_far, k_far, v_far, dk_far, dv_far,
        scratch=[pltpu.VMEM((padded, HDIM), F32)] * 2,
    )
    dkv_back = flipped(dkv_wire, 0, 1)
    dq_wire, dk_own, dv_own = call(
        high_own_kernel, (shape(rows, 640), grad, grad),
        high_far, q_s, do_s, k_own, v_own, dq_low, dq_high, dk_own, dv_own,
    )
    dq_back = flipped(dq_wire, 0, 4)
    own_g = call(own_grads_kernel, shape(4, rows, 512, dtype=F32), dq_own, dk_own, dv_own)
    packed_g = call(pack_grads_kernel, shape(4, rows, 512), own_g, dkv_back, dq_back)
    held = [packed_g[0]] + to_chips(packed_g)
    other = [flipped(a[:, 256:], 1, 0) for a in held]
    out = shape(rows, queries.shape[2])
    grads = call(
        unpack_grads_kernel, (out, out, out), *held, *other,
        scratch=[pltpu.VMEM((4, rows, 256), BF16)] * 2,
    )
    return tuple(grad[None] for grad in grads)


def solution(mesh):
    placed = P(None, ("blk", "head"), None)
    on_grid = mesh.shape["head"] == 4 and mesh.shape["blk"] == 8
    return jax.shard_map(
        grid_body if on_grid else ring_body,
        mesh=mesh,
        in_specs=(placed,) * 5 + (P(None, "head", "blk"),),
        out_specs=(placed,) * 3,
        check_vma=False,
    )
```

```python
import functools
import math

import jax
import jax.numpy as jnp
from jax import lax
from jax.experimental import pallas as pl
from jax.experimental.pallas import tpu as pltpu
from jax.sharding import PartitionSpec as P

HDIM = 80
SCALING = HDIM ** (-0.5)
LOG2E = math.log2(math.e)
PADDED = 96
LOW = 3
LOW_KEYS = 3
VMEM_LIMIT = 24 * 1024 * 1024
F32 = jnp.float32
BF16 = jnp.bfloat16


def shifted(block, axis, distance):
    devices = range(lax.axis_size(axis))
    route = [((i - distance) % len(devices), i) for i in devices]
    return lax.ppermute(block, axis, route)


def tile_terms(query_h, cotan_h, lse_rows, delta_rows, key_h, value_h):
    query_rows = query_h.shape[0]
    key_rows = key_h.shape[0]
    groups = query_h.shape[1]
    scores = (
        jnp.einsum("qhd,khd->hqk", query_h, key_h, preferred_element_type=jnp.float32) * SCALING
    )
    probs = jnp.exp(scores - lse_rows[:, :, None])
    probs16 = probs.astype(jnp.bfloat16)
    value_part = jnp.einsum("hqk,qhd->khd", probs16, cotan_h, preferred_element_type=jnp.float32)
    dprobs = jnp.einsum("qhd,khd->hqk", cotan_h, value_h, preferred_element_type=jnp.float32)
    dscores = (probs * (dprobs - delta_rows[:, :, None])).astype(jnp.bfloat16)
    query_part = jnp.einsum("hqk,khd->qhd", dscores, key_h, preferred_element_type=jnp.float32)
    key_part = jnp.einsum("hqk,qhd->khd", dscores, query_h, preferred_element_type=jnp.float32)
    return (
        query_part.reshape(query_rows, groups * HDIM),
        key_part.reshape(key_rows, groups * HDIM),
        value_part.reshape(key_rows, groups * HDIM),
    )


def crop_terms(query_h, cotan_h, lse_rows, delta_rows, key_h, value_h):
    return lax.map(
        lambda pieces: tile_terms(*pieces), (query_h, cotan_h, lse_rows, delta_rows, key_h, value_h)
    )


def ring_body(queries, keys, values, outputs, grad_out, lse):
    crops = queries.shape[0]
    groups = lse.shape[1]
    rows = lse.shape[2]
    query_own, key_own, value_own, cotan_own, output_own = (
        lax.all_to_all(sent, "head", split_axis=2, concat_axis=1, tiled=True)
        for sent in (queries, keys, values, grad_out, outputs)
    )
    products = cotan_own.astype(jnp.float32) * output_own.astype(jnp.float32)
    delta_rows = jnp.transpose(
        jnp.sum(products.reshape(crops, rows, groups, HDIM), axis=-1), (0, 2, 1)
    )
    query_h = query_own.reshape(crops, rows, groups, HDIM)
    cotan_h = cotan_own.reshape(crops, rows, groups, HDIM)
    key_h = key_own.reshape(crops, rows, groups, HDIM)
    value_h = value_own.reshape(crops, rows, groups, HDIM)
    width = groups * HDIM
    nblocks = lax.axis_size("blk")
    zeros_acc = jnp.zeros((crops, rows, width), jnp.float32)
    start = (query_h, cotan_h, lse, delta_rows, zeros_acc, zeros_acc, zeros_acc)

    def cycle_step(index, carry):
        query_cur, cotan_cur, lse_cur, delta_cur, query_acc, key_acc, value_acc = carry
        query_part, key_part, value_part = crop_terms(
            query_cur, cotan_cur, lse_cur, delta_cur, key_h, value_h
        )
        query_acc, lse_cur, delta_cur = shifted(
            (query_acc + query_part, lse_cur, delta_cur), "blk", 1
        )
        query_cur, cotan_cur = shifted((query_cur, cotan_cur), "blk", 1)
        return (
            query_cur,
            cotan_cur,
            lse_cur,
            delta_cur,
            query_acc,
            key_acc + key_part,
            value_acc + value_part,
        )

    query_cur, cotan_cur, lse_cur, delta_cur, query_acc, key_acc, value_acc = lax.fori_loop(
        0, nblocks - 1, cycle_step, start
    )
    query_part, key_part, value_part = crop_terms(
        query_cur, cotan_cur, lse_cur, delta_cur, key_h, value_h
    )
    query_total = shifted((query_acc + query_part).astype(jnp.bfloat16), "blk", 1).astype(
        jnp.float32
    )
    grad_q16 = (query_total * SCALING).astype(jnp.bfloat16)
    grad_k16 = ((key_acc + key_part) * SCALING).astype(jnp.bfloat16)
    grad_v16 = (value_acc + value_part).astype(jnp.bfloat16)
    return tuple(
        lax.all_to_all(grad, "head", split_axis=1, concat_axis=2, tiled=True)
        for grad in (grad_q16, grad_k16, grad_v16)
    )


def call(kernel, out_shape, *operands, scratch=(), remote=0, out_space=pltpu.VMEM, limit=VMEM_LIMIT):
    specs = [
        pl.BlockSpec(memory_space=pltpu.HBM if i < remote else pltpu.VMEM)
        for i in range(len(operands))
    ]
    return pl.pallas_call(
        kernel,
        out_shape=out_shape,
        in_specs=specs,
        out_specs=jax.tree.map(lambda _: pl.BlockSpec(memory_space=out_space), out_shape),
        scratch_shapes=list(scratch),
        compiler_params=pltpu.CompilerParams(vmem_limit_bytes=limit),
    )(*operands)


def place():
    h, b = lax.axis_index("head"), lax.axis_index("blk")
    return lax.div(h, 2), lax.rem(lax.div(b, 2), 2), lax.rem(h, 2), h


def shape(*dims, dtype=BF16):
    return jax.ShapeDtypeStruct(dims, dtype)


def head_of(array, head):
    return array[:, HDIM * head : HDIM * (head + 1)]


def pieces_of(row):
    high = row.astype(BF16)
    rest = row - high.astype(F32)
    middle = rest.astype(BF16)
    low = (rest - middle.astype(F32)).astype(BF16)
    return jnp.concatenate([high.astype(F32), middle.astype(F32), low.astype(F32)], axis=0)


def pack_inputs_kernel(
    q_in, k_in, v_in, o_in, do_in, lse_in, out0, out1, out2, out3,
    q_s, k_s, v_s, o_s, do_s, lse_s, out_ref, done, sent,
):
    x, w, c, _ = place()
    copies = [
        pltpu.make_async_copy(source, target, done.at[i])
        for i, (source, target) in enumerate(
            (source.at[spot], target.at[spot])
            for source, target in ((q_in, q_s), (do_in, do_s), (k_in, k_s), (v_in, v_s), (o_in, o_s))
            for spot in (pl.ds(0, 48), pl.ds(48, 40))
        )
    ] + [pltpu.make_async_copy(lse_in, lse_s, done.at[10])]
    for copy in copies:
        copy.start()
    for copy in copies[:8]:
        copy.wait()
    rows = q_s.shape[0]
    q, k, v, do = q_s[...], k_s[...], v_s[...], do_s[...]
    outs = (out0, out1, out2, out3)

    def leave(part, spot):
        return [
            pltpu.make_async_copy(out_ref.at[j, spot], out.at[spot], sent.at[4 * part + j])
            for j, out in enumerate(outs)
        ]

    for side in range(2):

        @pl.when(c == side)
        def _():
            for xs in range(2):
                for ws in range(2):
                    near, deep = [], []
                    for cs in (side, 1 - side):
                        head = 4 * xs + 2 * cs + ws
                        value = head_of(v, head)
                        near += [head_of(q, head), head_of(do, head), head_of(k, head), value[:, :16]]
                        deep.append(value[:, 16:])
                    j = 2 * (x ^ xs) + (w ^ ws)
                    out_ref[j, 0:rows] = jnp.concatenate(near + deep, axis=1)

    most = leave(0, pl.ds(0, PADDED - 16))
    for copy in most:
        copy.start()
    for copy in copies[8:]:
        copy.wait()
    products = do.astype(F32) * o_s[...].astype(F32)
    high = products.astype(BF16)
    rest = products - high.astype(F32)
    middle = rest.astype(BF16)
    low = (rest - middle.astype(F32)).astype(BF16)
    row = lax.broadcasted_iota(jnp.int32, (8, 640), 0)
    lane = lax.broadcasted_iota(jnp.int32, (8, 640), 1)
    mine = jnp.where((lane >= HDIM * row) & (lane < HDIM * (row + 1)), 1.0, 0.0).astype(BF16)
    deltas = sum(
        lax.dot_general(mine, part, (((1,), (1,)), ((), ())), preferred_element_type=F32)
        for part in (low, middle, high)
    )
    lse = lse_s[pl.ds(1 - w, 1), :] * LOG2E
    lse = jnp.concatenate([lse[:, rows * i : rows * (i + 1)] for i in range(4)], axis=0)
    lse = pieces_of(lse)
    blank = jnp.zeros((3, 128 - rows), F32)
    gap = jnp.zeros((5, 128), F32)
    edge = jnp.zeros((8, 128 - rows), F32)
    sides = [
        jnp.concatenate([lse[0:8], edge], axis=1),
        jnp.concatenate([jnp.concatenate([lse[8:12], lse[8:12]], axis=0), edge], axis=1),
    ]
    for xs in range(2):
        for ws in range(2):
            j = 2 * (x ^ xs) + (w ^ ws)
            pair = []
            for cs in range(2):
                head = 4 * xs + 2 * cs + ws
                delta = jnp.concatenate([pieces_of(deltas[head : head + 1, :]), blank], axis=1)
                pair.append(jnp.concatenate([delta, gap], axis=0))
            kept = jnp.where(c == 0, pair[0], pair[1])
            given = jnp.where(c == 0, pair[1], pair[0])
            spots = [kept, sides[0], given, sides[1], jnp.zeros((8, 128), F32)]
            out_ref[j, rows:PADDED] = jnp.concatenate(spots, axis=1).astype(BF16)
    last = leave(1, pl.ds(PADDED - 16, 16))
    for copy in last:
        copy.start()
    for copy in most + last:
        copy.wait()


def gather_queries_kernel(spots, *refs):
    *parts, near1, lse_in, wire, lse_s = refs
    rows = PADDED - 8
    _, w, _, h = place()
    own = lse_in[pl.ds(w, 1), :] * LOG2E
    below = near1[rows:PADDED, :].astype(F32)
    near = below[0:4, 128 : 128 + rows] + below[4:8, 128 : 128 + rows]
    near = near + below[0:4, 384 : 384 + rows]
    lse_s[...] = jnp.concatenate(
        [own[:, rows * i : rows * (i + 1)] for i in range(4)] + [near], axis=0
    )
    lower = []
    gap = jnp.zeros((6, PADDED - rows), F32)
    for (j, r), ref in zip(spots, parts):
        delta = ref[rows:PADDED, 0:128].astype(F32)[0:3, 0:rows]
        lse = lse_s[pl.ds(4 * (j % 2) + (h ^ (2 * (j // 2) + r)), 1), :]
        lower += [jnp.concatenate([delta, pieces_of(lse)], axis=0), gap]
    wire[0:rows] = jnp.concatenate([ref[0:rows, 0:160] for ref in parts], axis=1)
    width = wire.shape[1] - len(parts) * PADDED
    lower = jnp.concatenate(lower + [jnp.zeros((6, width), F32)], axis=1)
    lower = jnp.concatenate([lower, jnp.zeros((2, wire.shape[1]), F32)], axis=0)
    wire[rows:PADDED] = lower.astype(BF16)


def gather_keys_kernel(spots, *refs):
    *parts, keys = refs
    rows = PADDED - 8
    pieces = []
    for (_, r), ref in zip(spots, parts):
        deep = 320 if r else 512
        pieces += [ref[0:rows, 160:256], ref[0:rows, deep : deep + 64]]
    keys[0:rows] = jnp.concatenate(pieces, axis=1)
    if keys.shape[0] > rows:
        keys[rows:PADDED] = jnp.zeros((PADDED - rows, keys.shape[1]), BF16)


def rows_of(wires):
    rows = PADDED - 8
    below = jnp.concatenate(
        [
            wire[rows:PADDED, 0 : wire.shape[1] // (2 * HDIM) * PADDED].astype(F32)
            for wire in wires
        ],
        axis=1,
    )
    return below[3:4] + below[4:5] + below[5:6], below[0:1] + below[1:2] + below[2:3]


def spread(wide, left, right, first=0):
    rows = PADDED - 8
    blank = jnp.zeros((16, HDIM), BF16)
    for i in range(wide.shape[1] // (2 * HDIM)):
        at, lane = PADDED * (first + i), 2 * HDIM * i
        for target, start in ((left, lane), (right, lane + HDIM)):
            target[pl.ds(at + PADDED - 16, 16), :] = blank
            target[pl.ds(at, rows), :] = wide[0:rows, start : start + HDIM]


def tile_step(q, do, k_s, v_s, lse, delta, chunk=768):
    q_t, do_t = q.T, do.T
    k_t = k_s[...].T
    dq_t = None
    parts = []
    for start in range(0, k_s.shape[0], chunk):
        spot = slice(start, start + chunk)
        k, v = k_s[spot, :], v_s[spot, :]
        scores = jnp.dot(k, q_t, preferred_element_type=F32)
        probs = jnp.exp2(scores * (SCALING * LOG2E) - lse)
        dv = jnp.dot(probs.astype(BF16), do, preferred_element_type=F32)
        dprobs = jnp.dot(v, do_t, preferred_element_type=F32)
        dscores = (probs * (dprobs - delta)).astype(BF16)
        dk = jnp.dot(dscores, q, preferred_element_type=F32)
        more = jnp.dot(k_t[:, spot], dscores, preferred_element_type=F32)
        dq_t = more if dq_t is None else dq_t + more
        parts.append((spot, dk, dv))
    return dq_t, parts


def to_wire(arrays, rows):
    count = arrays[0].shape[0] // PADDED
    return jnp.concatenate(
        [a[PADDED * i : PADDED * i + rows].astype(BF16) for i in range(count) for a in arrays],
        axis=1,
    )


def own_own_kernel(low, high, k_low, k_high, dq_t, dk, dv, q_s, do_s, k_s, v_s):
    spread(low, q_s, do_s)
    spread(high, q_s, do_s, LOW)
    spread(k_low, k_s, v_s)
    spread(k_high, k_s, v_s, LOW_KEYS)
    dq_t[...], parts = tile_step(q_s[...], do_s[...], k_s, v_s, *rows_of([low, high]))
    for spot, dk_part, dv_part in parts:
        dk[spot, :] = dk_part
        dv[spot, :] = dv_part


def own_far_kernel(after, low, high, q_s, do_s, k_low, k_high, dq_before, dq_t, dk, dv, k_s, v_s):
    spread(k_low, k_s, v_s)
    spread(k_high, k_s, v_s, LOW_KEYS)
    more, parts = tile_step(q_s[...], do_s[...], k_s, v_s, *rows_of([low, high]))
    dq_t[...] = dq_before[...] + more
    for spot, dk_part, dv_part in parts:
        dk[spot, :] = dk_part
        dv[spot, :] = dv_part


def low_own_kernel(wire, k_own, v_own, dk_in, dv_in, dq_t, dk, dv, q_s, do_s):
    spread(wire, q_s, do_s)
    dq_t[...], parts = tile_step(q_s[...], do_s[...], k_own, v_own, *rows_of([wire]))
    for spot, dk_part, dv_part in parts:
        dk[spot, :] = dk_in[spot, :] + dk_part
        dv[spot, :] = dv_in[spot, :] + dv_part


def low_far_kernel(wire, q_s, do_s, k_far, v_far, dq_before, dk_in, dv_in, dq_t, dk, dv):
    more, parts = tile_step(q_s[...], do_s[...], k_far, v_far, *rows_of([wire]))
    dq_t[...] = dq_before[...] + more
    for spot, dk_part, dv_part in parts:
        dk[spot, :] = dk_in[spot, :] + dk_part
        dv[spot, :] = dv_in[spot, :] + dv_part


def high_kernel(
    wire, k_far, v_far, k_own, v_own, dk_far, dv_far, dq_low, dk_in, dv_in,
    dkv_wire, dq_wire, dk_own, dv_own, q_s, do_s, dk, dv,
):
    spread(wire, q_s, do_s)
    q, do = q_s[...], do_s[...]
    rows = rows_of([wire])
    first, parts = tile_step(q, do, k_far, v_far, *rows)
    for spot, dk_part, dv_part in parts:
        dk[spot, :] = (dk_far[spot, :] + dk_part) * SCALING
        dv[spot, :] = dv_far[spot, :] + dv_part
    dkv_wire[...] = to_wire([dk[...], dv[...]], dkv_wire.shape[0])
    more, parts = tile_step(q, do, k_own, v_own, *rows)
    dq = jnp.concatenate([dq_low[...], first + more], axis=1) * SCALING
    dq_wire[...] = to_wire([dq.T], dq_wire.shape[0])
    for spot, dk_part, dv_part in parts:
        dk_own[spot, :] = dk_in[spot, :] + dk_part
        dv_own[spot, :] = dv_in[spot, :] + dv_part


def own_grads_kernel(dq_t, dk, dv, out):
    rows = out.shape[1]
    dq = dq_t[...].T * SCALING
    zeros = jnp.zeros((rows, 16), F32)
    for i in range(8):
        spot = slice(PADDED * i, PADDED * i + rows)
        block = jnp.concatenate([dq[spot], dk[spot, :] * SCALING, dv[spot, :], zeros], axis=1)
        out[i // 2, :, 256 * (i % 2) : 256 * (i % 2) + 256] = block


def pack_grads_kernel(own, dkv_wire, dq_wire, out):
    rows = dkv_wire.shape[0]
    dq = dq_wire[...]
    dkv = dkv_wire[...]
    zeros = jnp.zeros((rows, 16), BF16)
    for i in range(8):
        block = jnp.concatenate(
            [
                dq[:, HDIM * i : HDIM * (i + 1)],
                dkv[:, 2 * HDIM * i : 2 * HDIM * (i + 1)],
                zeros,
            ],
            axis=1,
        )
        lanes = slice(256 * (i % 2), 256 * (i % 2) + 256)
        out[i // 2, :, lanes] = (own[i // 2, :, lanes] + block.astype(F32)).astype(BF16)


def unpack_grads_kernel(*refs):
    kept, given, dq, dk, dv, held, other = refs[0:4], refs[4:8], *refs[8:]
    x, w, c, _ = place()
    for j in range(4):
        held[j] = kept[j][:, 0:256]
        other[j] = given[j][...]
    blocks = []
    for head in range(8):
        xs, cs, ws = head // 4, (head // 2) % 2, head % 2
        j = 2 * (x ^ xs) + (w ^ ws)
        blocks.append(jnp.where(c == cs, held[j].astype(F32), other[j].astype(F32)).astype(BF16))
    for k, out in enumerate((dq, dk, dv)):
        out[...] = jnp.concatenate(
            [block[:, HDIM * k : HDIM * (k + 1)] for block in blocks], axis=1
        )


def flipped(array, head_bits, blk_bits):
    heads, blks = lax.axis_size("head"), lax.axis_size("blk")
    if not blk_bits:
        return lax.ppermute(array, "head", [(i, i ^ head_bits) for i in range(heads)])
    if not head_bits:
        return lax.ppermute(array, "blk", [(i, i ^ blk_bits) for i in range(blks)])
    bits = head_bits * blks + blk_bits
    return lax.ppermute(array, ("head", "blk"), [(i, i ^ bits) for i in range(heads * blks)])


def to_chips(packed):
    return [flipped(packed[1], 0, 2), flipped(packed[2], 2, 0), flipped(packed[3], 2, 2)]


def grid_body(queries, keys, values, outputs, grad_out, lse):
    rows = queries.shape[1]
    padded = 8 * PADDED
    few = LOW * PADDED

    packed = call(
        pack_inputs_kernel,
        (shape(PADDED, 640),) * 4,
        queries[0], keys[0], values[0], outputs[0], grad_out[0], lse[0],
        remote=6,
        out_space=pltpu.HBM,
        limit=57 * 1024 * 1024,
        scratch=[pltpu.VMEM(queries.shape[1:], BF16)] * 5
        + [pltpu.VMEM(lse.shape[1:], F32), pltpu.VMEM((4, PADDED, 640), BF16)]
        + [pltpu.SemaphoreType.DMA((11,)), pltpu.SemaphoreType.DMA((8,))],
    )
    own = packed[0]
    near = to_chips(packed)
    other = [flipped(a[:, 256:], 1, 0) for a in [own] + near]
    blocks = [ref for pair in zip([own] + near, other) for ref in pair]
    spots = [(j, r) for j in range(4) for r in range(2)]

    def gather_queries(first, last):
        return call(
            functools.partial(gather_queries_kernel, spots[first:last]),
            shape(PADDED, 160 * (last - first)),
            *blocks[first:last], near[0], lse[0],
            scratch=[pltpu.VMEM((8, rows), F32)],
        )

    def gather_keys(first, last, tall):
        return call(
            functools.partial(gather_keys_kernel, spots[first:last]),
            shape(tall, 160 * (last - first)),
            *blocks[first:last],
        )

    low, k_low = gather_queries(0, LOW), gather_keys(0, LOW_KEYS, PADDED)
    low_far, k_low_far = flipped(low, 0, 4), flipped(k_low, 0, 1)
    high, k_high = gather_queries(LOW, 8), gather_keys(LOW_KEYS, 8, rows)
    high_far = flipped(high, 0, 4)
    k_high, k_low_far, low_far = lax.optimization_barrier((k_high, k_low_far, low_far))
    k_high_far = flipped(k_high, 0, 1)
    keys_far = [k_low_far, k_high_far]

    grad = shape(padded, HDIM, dtype=F32)
    side = shape(padded, HDIM)
    dq_shape = shape(HDIM, padded, dtype=F32)
    dq_own, dk_own, dv_own, q_s, do_s, k_own, v_own = call(
        own_own_kernel, (dq_shape, grad, grad, side, side, side, side), low, high, k_low, k_high
    )
    some = shape(few, HDIM)
    dq_low, dk_own, dv_own, q_low_s, do_low_s = call(
        low_own_kernel, (shape(HDIM, few, dtype=F32), grad, grad, some, some),
        low_far, k_own, v_own, dk_own, dv_own,
    )
    dq_own, dk_far, dv_far, k_far, v_far = call(
        own_far_kernel, (dq_shape, grad, grad, side, side),
        dq_low, low, high, q_s, do_s, *keys_far, dq_own,
    )
    dq_low, dk_far, dv_far = call(
        low_far_kernel, (shape(HDIM, few, dtype=F32), grad, grad),
        low_far, q_low_s, do_low_s, k_far, v_far, dq_low, dk_far, dv_far,
    )
    dkv_wire, dq_wire, dk_own, dv_own = call(
        high_kernel, (shape(rows, 1280), shape(rows, 640), grad, grad),
        high_far, k_far, v_far, k_own, v_own, dk_far, dv_far, dq_low, dk_own, dv_own,
        scratch=[pltpu.VMEM((padded - few, HDIM), BF16)] * 2 + [pltpu.VMEM((padded, HDIM), F32)] * 2,
    )
    dkv_back = flipped(dkv_wire, 0, 1)
    dq_back = flipped(dq_wire, 0, 4)
    own_g = call(own_grads_kernel, shape(4, rows, 512, dtype=F32), dq_own, dk_own, dv_own)
    packed_g = call(pack_grads_kernel, shape(4, rows, 512), own_g, dkv_back, dq_back)
    held = [packed_g[0]] + to_chips(packed_g)
    other = [flipped(a[:, 256:], 1, 0) for a in held]
    out = shape(rows, queries.shape[2])
    grads = call(
        unpack_grads_kernel, (out, out, out), *held, *other,
        scratch=[pltpu.VMEM((4, rows, 256), BF16)] * 2,
    )
    return tuple(grad[None] for grad in grads)


def solution(mesh):
    placed = P(None, ("blk", "head"), None)
    on_grid = mesh.shape["head"] == 4 and mesh.shape["blk"] == 8
    return jax.shard_map(
        grid_body if on_grid else ring_body,
        mesh=mesh,
        in_specs=(placed,) * 5 + (P(None, "head", "blk"),),
        out_specs=(placed,) * 3,
        check_vma=False,
    )
```

```python
import functools
import math

import jax
import jax.numpy as jnp
from jax import lax
from jax.experimental import pallas as pl
from jax.experimental.pallas import tpu as pltpu
from jax.sharding import PartitionSpec as P

HDIM = 80
SCALING = HDIM ** (-0.5)
LOG2E = math.log2(math.e)
PADDED = 96
LOW = 3
LOW_KEYS = 3
VMEM_LIMIT = 24 * 1024 * 1024
F32 = jnp.float32
BF16 = jnp.bfloat16


def shifted(block, axis, distance):
    devices = range(lax.axis_size(axis))
    route = [((i - distance) % len(devices), i) for i in devices]
    return lax.ppermute(block, axis, route)


def tile_terms(query_h, cotan_h, lse_rows, delta_rows, key_h, value_h):
    query_rows = query_h.shape[0]
    key_rows = key_h.shape[0]
    groups = query_h.shape[1]
    scores = (
        jnp.einsum("qhd,khd->hqk", query_h, key_h, preferred_element_type=jnp.float32) * SCALING
    )
    probs = jnp.exp(scores - lse_rows[:, :, None])
    probs16 = probs.astype(jnp.bfloat16)
    value_part = jnp.einsum("hqk,qhd->khd", probs16, cotan_h, preferred_element_type=jnp.float32)
    dprobs = jnp.einsum("qhd,khd->hqk", cotan_h, value_h, preferred_element_type=jnp.float32)
    dscores = (probs * (dprobs - delta_rows[:, :, None])).astype(jnp.bfloat16)
    query_part = jnp.einsum("hqk,khd->qhd", dscores, key_h, preferred_element_type=jnp.float32)
    key_part = jnp.einsum("hqk,qhd->khd", dscores, query_h, preferred_element_type=jnp.float32)
    return (
        query_part.reshape(query_rows, groups * HDIM),
        key_part.reshape(key_rows, groups * HDIM),
        value_part.reshape(key_rows, groups * HDIM),
    )


def crop_terms(query_h, cotan_h, lse_rows, delta_rows, key_h, value_h):
    return lax.map(
        lambda pieces: tile_terms(*pieces), (query_h, cotan_h, lse_rows, delta_rows, key_h, value_h)
    )


def ring_body(queries, keys, values, outputs, grad_out, lse):
    crops = queries.shape[0]
    groups = lse.shape[1]
    rows = lse.shape[2]
    query_own, key_own, value_own, cotan_own, output_own = (
        lax.all_to_all(sent, "head", split_axis=2, concat_axis=1, tiled=True)
        for sent in (queries, keys, values, grad_out, outputs)
    )
    products = cotan_own.astype(jnp.float32) * output_own.astype(jnp.float32)
    delta_rows = jnp.transpose(
        jnp.sum(products.reshape(crops, rows, groups, HDIM), axis=-1), (0, 2, 1)
    )
    query_h = query_own.reshape(crops, rows, groups, HDIM)
    cotan_h = cotan_own.reshape(crops, rows, groups, HDIM)
    key_h = key_own.reshape(crops, rows, groups, HDIM)
    value_h = value_own.reshape(crops, rows, groups, HDIM)
    width = groups * HDIM
    nblocks = lax.axis_size("blk")
    zeros_acc = jnp.zeros((crops, rows, width), jnp.float32)
    start = (query_h, cotan_h, lse, delta_rows, zeros_acc, zeros_acc, zeros_acc)

    def cycle_step(index, carry):
        query_cur, cotan_cur, lse_cur, delta_cur, query_acc, key_acc, value_acc = carry
        query_part, key_part, value_part = crop_terms(
            query_cur, cotan_cur, lse_cur, delta_cur, key_h, value_h
        )
        query_acc, lse_cur, delta_cur = shifted(
            (query_acc + query_part, lse_cur, delta_cur), "blk", 1
        )
        query_cur, cotan_cur = shifted((query_cur, cotan_cur), "blk", 1)
        return (
            query_cur,
            cotan_cur,
            lse_cur,
            delta_cur,
            query_acc,
            key_acc + key_part,
            value_acc + value_part,
        )

    query_cur, cotan_cur, lse_cur, delta_cur, query_acc, key_acc, value_acc = lax.fori_loop(
        0, nblocks - 1, cycle_step, start
    )
    query_part, key_part, value_part = crop_terms(
        query_cur, cotan_cur, lse_cur, delta_cur, key_h, value_h
    )
    query_total = shifted((query_acc + query_part).astype(jnp.bfloat16), "blk", 1).astype(
        jnp.float32
    )
    grad_q16 = (query_total * SCALING).astype(jnp.bfloat16)
    grad_k16 = ((key_acc + key_part) * SCALING).astype(jnp.bfloat16)
    grad_v16 = (value_acc + value_part).astype(jnp.bfloat16)
    return tuple(
        lax.all_to_all(grad, "head", split_axis=1, concat_axis=2, tiled=True)
        for grad in (grad_q16, grad_k16, grad_v16)
    )


def call(kernel, out_shape, *operands, scratch=(), remote=0, out_space=pltpu.VMEM, limit=VMEM_LIMIT):
    specs = [
        pl.BlockSpec(memory_space=pltpu.HBM if i < remote else pltpu.VMEM)
        for i in range(len(operands))
    ]
    return pl.pallas_call(
        kernel,
        out_shape=out_shape,
        in_specs=specs,
        out_specs=jax.tree.map(lambda _: pl.BlockSpec(memory_space=out_space), out_shape),
        scratch_shapes=list(scratch),
        compiler_params=pltpu.CompilerParams(vmem_limit_bytes=limit),
    )(*operands)


def place():
    h, b = lax.axis_index("head"), lax.axis_index("blk")
    return lax.div(h, 2), lax.rem(lax.div(b, 2), 2), lax.rem(h, 2), h


def shape(*dims, dtype=BF16):
    return jax.ShapeDtypeStruct(dims, dtype)


def head_of(array, head):
    return array[:, HDIM * head : HDIM * (head + 1)]


def pieces_of(row):
    high = row.astype(BF16)
    rest = row - high.astype(F32)
    middle = rest.astype(BF16)
    low = (rest - middle.astype(F32)).astype(BF16)
    return jnp.concatenate([high.astype(F32), middle.astype(F32), low.astype(F32)], axis=0)


def pack_inputs_kernel(
    q_in, k_in, v_in, o_in, do_in, lse_in, out0, out1, out2, out3, give,
    q_s, k_s, v_s, o_s, do_s, lse_s, out_ref, done, sent,
):
    x, w, c, _ = place()
    copies = [
        pltpu.make_async_copy(source, target, done.at[i])
        for i, (source, target) in enumerate(
            ((q_in, q_s), (do_in, do_s), (k_in, k_s), (v_in, v_s), (o_in, o_s), (lse_in, lse_s))
        )
    ]
    for copy in copies:
        copy.start()
    for copy in copies[:4]:
        copy.wait()
    rows = q_s.shape[0]
    q, k, v, do = q_s[...], k_s[...], v_s[...], do_s[...]
    outs = (out0, out1, out2, out3)

    def leave(part, spot):
        mine = pltpu.make_async_copy(
            out_ref.at[0, spot, pl.ds(256, 384)], give.at[spot], sent.at[8 + part]
        )
        return [mine] + [
            pltpu.make_async_copy(out_ref.at[j, spot], out.at[spot], sent.at[4 * part + j])
            for j, out in enumerate(outs)
        ]

    for side in range(2):

        @pl.when(c == side)
        def _():
            for xs in range(2):
                for ws in range(2):
                    near, deep = [], []
                    for cs in (side, 1 - side):
                        head = 4 * xs + 2 * cs + ws
                        value = head_of(v, head)
                        near += [head_of(q, head), head_of(do, head), head_of(k, head), value[:, :16]]
                        deep.append(value[:, 16:])
                    j = 2 * (x ^ xs) + (w ^ ws)
                    out_ref[j, 0:rows] = jnp.concatenate(near + deep, axis=1)

    most = leave(0, pl.ds(0, PADDED - 16))
    for copy in most:
        copy.start()
    for copy in copies[4:]:
        copy.wait()
    products = do.astype(F32) * o_s[...].astype(F32)
    high = products.astype(BF16)
    rest = products - high.astype(F32)
    middle = rest.astype(BF16)
    low = (rest - middle.astype(F32)).astype(BF16)
    row = lax.broadcasted_iota(jnp.int32, (8, 640), 0)
    lane = lax.broadcasted_iota(jnp.int32, (8, 640), 1)
    mine = jnp.where((lane >= HDIM * row) & (lane < HDIM * (row + 1)), 1.0, 0.0).astype(BF16)
    deltas = sum(
        lax.dot_general(mine, part, (((1,), (1,)), ((), ())), preferred_element_type=F32)
        for part in (low, middle, high)
    )
    lse = lse_s[pl.ds(1 - w, 1), :] * LOG2E
    lse = jnp.concatenate([lse[:, rows * i : rows * (i + 1)] for i in range(4)], axis=0)
    lse = pieces_of(lse)
    blank = jnp.zeros((3, 128 - rows), F32)
    gap = jnp.zeros((5, 128), F32)
    edge = jnp.zeros((8, 128 - rows), F32)
    sides = [
        jnp.concatenate([lse[0:8], edge], axis=1),
        jnp.concatenate([jnp.concatenate([lse[8:12], lse[8:12]], axis=0), edge], axis=1),
    ]
    for xs in range(2):
        for ws in range(2):
            j = 2 * (x ^ xs) + (w ^ ws)
            pair = []
            for cs in range(2):
                head = 4 * xs + 2 * cs + ws
                delta = jnp.concatenate([pieces_of(deltas[head : head + 1, :]), blank], axis=1)
                pair.append(jnp.concatenate([delta, gap], axis=0))
            kept = jnp.where(c == 0, pair[0], pair[1])
            given = jnp.where(c == 0, pair[1], pair[0])
            spots = [kept, sides[0], given, sides[1], jnp.zeros((8, 128), F32)]
            out_ref[j, rows:PADDED] = jnp.concatenate(spots, axis=1).astype(BF16)
    last = leave(1, pl.ds(PADDED - 16, 16))
    for copy in last:
        copy.start()
    for copy in most + last:
        copy.wait()


def hold_kernel(block, held):
    held[...] = block[...]


def gather_queries_kernel(spots, *refs):
    *parts, near1, lse_in, wire, lse_s = refs
    rows = PADDED - 8
    _, w, _, h = place()
    own = lse_in[pl.ds(w, 1), :] * LOG2E
    below = near1[rows:PADDED, :].astype(F32)
    near = below[0:4, 128 : 128 + rows] + below[4:8, 128 : 128 + rows]
    near = near + below[0:4, 384 : 384 + rows]
    lse_s[...] = jnp.concatenate(
        [own[:, rows * i : rows * (i + 1)] for i in range(4)] + [near], axis=0
    )
    lower = []
    gap = jnp.zeros((6, PADDED - rows), F32)
    for (j, r), ref in zip(spots, parts):
        delta = ref[rows:PADDED, 0:128].astype(F32)[0:3, 0:rows]
        lse = lse_s[pl.ds(4 * (j % 2) + (h ^ (2 * (j // 2) + r)), 1), :]
        lower += [jnp.concatenate([delta, pieces_of(lse)], axis=0), gap]
    wire[0:rows] = jnp.concatenate([ref[0:rows, 0:160] for ref in parts], axis=1)
    width = wire.shape[1] - len(parts) * PADDED
    lower = jnp.concatenate(lower + [jnp.zeros((6, width), F32)], axis=1)
    lower = jnp.concatenate([lower, jnp.zeros((2, wire.shape[1]), F32)], axis=0)
    wire[rows:PADDED] = lower.astype(BF16)


def gather_keys_kernel(spots, *refs):
    *parts, keys = refs
    rows = PADDED - 8
    pieces = []
    for (_, r), ref in zip(spots, parts):
        deep = 320 if r else 512
        pieces += [ref[0:rows, 160:256], ref[0:rows, deep : deep + 64]]
    keys[0:rows] = jnp.concatenate(pieces, axis=1)
    if keys.shape[0] > rows:
        keys[rows:PADDED] = jnp.zeros((PADDED - rows, keys.shape[1]), BF16)


def rows_of(wires):
    rows = PADDED - 8
    below = jnp.concatenate(
        [
            wire[rows:PADDED, 0 : wire.shape[1] // (2 * HDIM) * PADDED].astype(F32)
            for wire in wires
        ],
        axis=1,
    )
    return below[3:4] + below[4:5] + below[5:6], below[0:1] + below[1:2] + below[2:3]


def spread(wide, left, right, first=0):
    rows = PADDED - 8
    blank = jnp.zeros((16, HDIM), BF16)
    for i in range(wide.shape[1] // (2 * HDIM)):
        at, lane = PADDED * (first + i), 2 * HDIM * i
        for target, start in ((left, lane), (right, lane + HDIM)):
            target[pl.ds(at + PADDED - 16, 16), :] = blank
            target[pl.ds(at, rows), :] = wide[0:rows, start : start + HDIM]


def tile_step(q, do, k_s, v_s, lse, delta, chunk=768):
    q_t, do_t = q.T, do.T
    k_t = k_s[...].T
    dq_t = None
    parts = []
    for start in range(0, k_s.shape[0], chunk):
        spot = slice(start, start + chunk)
        k, v = k_s[spot, :], v_s[spot, :]
        scores = jnp.dot(k, q_t, preferred_element_type=F32)
        probs = jnp.exp2(scores * (SCALING * LOG2E) - lse)
        dv = jnp.dot(probs.astype(BF16), do, preferred_element_type=F32)
        dprobs = jnp.dot(v, do_t, preferred_element_type=F32)
        dscores = (probs * (dprobs - delta)).astype(BF16)
        dk = jnp.dot(dscores, q, preferred_element_type=F32)
        more = jnp.dot(k_t[:, spot], dscores, preferred_element_type=F32)
        dq_t = more if dq_t is None else dq_t + more
        parts.append((spot, dk, dv))
    return dq_t, parts


def to_wire(arrays, rows):
    count = arrays[0].shape[0] // PADDED
    return jnp.concatenate(
        [a[PADDED * i : PADDED * i + rows].astype(BF16) for i in range(count) for a in arrays],
        axis=1,
    )


def own_own_kernel(low, high, k_low, k_high, dq_t, dk, dv, q_s, do_s, k_s, v_s):
    spread(low, q_s, do_s)
    spread(high, q_s, do_s, LOW)
    spread(k_low, k_s, v_s)
    spread(k_high, k_s, v_s, LOW_KEYS)
    dq_t[...], parts = tile_step(q_s[...], do_s[...], k_s, v_s, *rows_of([low, high]))
    for spot, dk_part, dv_part in parts:
        dk[spot, :] = dk_part
        dv[spot, :] = dv_part


def low_own_kernel(wire, k_own, v_own, dk_in, dv_in, dq_t, dk, dv, q_s, do_s):
    spread(wire, q_s, do_s)
    dq_t[...], parts = tile_step(q_s[...], do_s[...], k_own, v_own, *rows_of([wire]))
    for spot, dk_part, dv_part in parts:
        dk[spot, :] = dk_in[spot, :] + dk_part
        dv[spot, :] = dv_in[spot, :] + dv_part


def far_keys_kernel(
    low, high, low_far, q_s, do_s, q_low_s, do_low_s, k_low, k_high, dq_before, dq_low_before,
    dq_t, dq_low, dk, dv, k_s, v_s, all_q, all_do,
):
    spread(k_low, k_s, v_s)
    spread(k_high, k_s, v_s, LOW_KEYS)
    own = q_s.shape[0]
    all_q[0:own], all_q[own:] = q_s[...], q_low_s[...]
    all_do[0:own], all_do[own:] = do_s[...], do_low_s[...]
    more, parts = tile_step(
        all_q[...], all_do[...], k_s, v_s, *rows_of([low, high, low_far])
    )
    dq_t[...] = dq_before[...] + more[:, 0:own]
    dq_low[...] = dq_low_before[...] + more[:, own:]
    for spot, dk_part, dv_part in parts:
        dk[spot, :] = dk_part
        dv[spot, :] = dv_part


def high_kernel(
    wire, k_far, v_far, k_own, v_own, dk_far, dv_far, dq_low, dk_in, dv_in,
    dkv_wire, dq_wire, dk_own, dv_own, q_s, do_s, dk, dv,
):
    spread(wire, q_s, do_s)
    q, do = q_s[...], do_s[...]
    rows = rows_of([wire])
    first, parts = tile_step(q, do, k_far, v_far, *rows)
    for spot, dk_part, dv_part in parts:
        dk[spot, :] = (dk_far[spot, :] + dk_part) * SCALING
        dv[spot, :] = dv_far[spot, :] + dv_part
    dkv_wire[...] = to_wire([dk[...], dv[...]], dkv_wire.shape[0])
    more, parts = tile_step(q, do, k_own, v_own, *rows)
    dq = jnp.concatenate([dq_low[...], first + more], axis=1) * SCALING
    dq_wire[...] = to_wire([dq.T], dq_wire.shape[0])
    for spot, dk_part, dv_part in parts:
        dk_own[spot, :] = dk_in[spot, :] + dk_part
        dv_own[spot, :] = dv_in[spot, :] + dv_part


def own_grads_kernel(dq_t, dk, dv, out):
    rows = out.shape[1]
    dq = dq_t[...].T * SCALING
    zeros = jnp.zeros((rows, 16), F32)
    for i in range(8):
        spot = slice(PADDED * i, PADDED * i + rows)
        block = jnp.concatenate([dq[spot], dk[spot, :] * SCALING, dv[spot, :], zeros], axis=1)
        out[i // 2, :, 256 * (i % 2) : 256 * (i % 2) + 256] = block


def pack_grads_kernel(own, dkv_wire, dq_wire, out):
    rows = dkv_wire.shape[0]
    dq = dq_wire[...]
    dkv = dkv_wire[...]
    zeros = jnp.zeros((rows, 16), BF16)
    for i in range(8):
        block = jnp.concatenate(
            [
                dq[:, HDIM * i : HDIM * (i + 1)],
                dkv[:, 2 * HDIM * i : 2 * HDIM * (i + 1)],
                zeros,
            ],
            axis=1,
        )
        lanes = slice(256 * (i % 2), 256 * (i % 2) + 256)
        out[i // 2, :, lanes] = (own[i // 2, :, lanes] + block.astype(F32)).astype(BF16)


def unpack_grads_kernel(*refs):
    kept, given, dq, dk, dv, held, other = refs[0:4], refs[4], *refs[5:]
    x, w, c, _ = place()
    for j in range(4):
        held[j] = kept[j][:, 0:256]
        other[j] = given[j]
    blocks = []
    for head in range(8):
        xs, cs, ws = head // 4, (head // 2) % 2, head % 2
        j = 2 * (x ^ xs) + (w ^ ws)
        blocks.append(jnp.where(c == cs, held[j].astype(F32), other[j].astype(F32)).astype(BF16))
    for k, out in enumerate((dq, dk, dv)):
        out[...] = jnp.concatenate(
            [block[:, HDIM * k : HDIM * (k + 1)] for block in blocks], axis=1
        )


def flipped(array, head_bits, blk_bits):
    heads, blks = lax.axis_size("head"), lax.axis_size("blk")
    if not blk_bits:
        return lax.ppermute(array, "head", [(i, i ^ head_bits) for i in range(heads)])
    if not head_bits:
        return lax.ppermute(array, "blk", [(i, i ^ blk_bits) for i in range(blks)])
    bits = head_bits * blks + blk_bits
    return lax.ppermute(array, ("head", "blk"), [(i, i ^ bits) for i in range(heads * blks)])


def to_chips(packed):
    return [flipped(packed[1], 0, 2), flipped(packed[2], 2, 0), flipped(packed[3], 2, 2)]


def grid_body(queries, keys, values, outputs, grad_out, lse):
    rows = queries.shape[1]
    padded = 8 * PADDED
    few = LOW * PADDED

    packed = call(
        pack_inputs_kernel,
        (shape(PADDED, 640),) * 4 + (shape(PADDED, 384),),
        queries[0], keys[0], values[0], outputs[0], grad_out[0], lse[0],
        remote=6,
        out_space=pltpu.HBM,
        limit=57 * 1024 * 1024,
        scratch=[pltpu.VMEM(queries.shape[1:], BF16)] * 5
        + [pltpu.VMEM(lse.shape[1:], F32), pltpu.VMEM((4, PADDED, 640), BF16)]
        + [pltpu.SemaphoreType.DMA((6,)), pltpu.SemaphoreType.DMA((10,))],
    )
    own = call(hold_kernel, shape(PADDED, 640), packed[0])
    near = to_chips(packed)
    other = [flipped(a, 1, 0) for a in [packed[4]] + [b[:, 256:] for b in near]]
    blocks = [ref for pair in zip([own] + near, other) for ref in pair]
    spots = [(j, r) for j in range(4) for r in range(2)]

    def gather_queries(first, last):
        return call(
            functools.partial(gather_queries_kernel, spots[first:last]),
            shape(PADDED, 160 * (last - first)),
            *blocks[first:last], near[0], lse[0],
            scratch=[pltpu.VMEM((8, rows), F32)],
        )

    def gather_keys(first, last, tall):
        return call(
            functools.partial(gather_keys_kernel, spots[first:last]),
            shape(tall, 160 * (last - first)),
            *blocks[first:last],
        )

    low, k_low = gather_queries(0, LOW), gather_keys(0, LOW_KEYS, PADDED)
    low_far, k_low_far = flipped(low, 0, 4), flipped(k_low, 0, 1)
    high, k_high = gather_queries(LOW, 8), gather_keys(LOW_KEYS, 8, rows)
    high_far = flipped(high, 0, 4)
    k_high, k_low_far, low_far = lax.optimization_barrier((k_high, k_low_far, low_far))
    k_high_far = flipped(k_high, 0, 1)
    keys_far = [k_low_far, k_high_far]

    grad = shape(padded, HDIM, dtype=F32)
    side = shape(padded, HDIM)
    dq_shape = shape(HDIM, padded, dtype=F32)
    dq_own, dk_own, dv_own, q_s, do_s, k_own, v_own = call(
        own_own_kernel, (dq_shape, grad, grad, side, side, side, side), low, high, k_low, k_high
    )
    some = shape(few, HDIM)
    dq_low, dk_own, dv_own, q_low_s, do_low_s = call(
        low_own_kernel, (shape(HDIM, few, dtype=F32), grad, grad, some, some),
        low_far, k_own, v_own, dk_own, dv_own,
    )
    dq_own, dq_low, dk_far, dv_far, k_far, v_far = call(
        far_keys_kernel, (dq_shape, shape(HDIM, few, dtype=F32), grad, grad, side, side),
        low, high, low_far, q_s, do_s, q_low_s, do_low_s, *keys_far, dq_own, dq_low,
        scratch=[pltpu.VMEM((padded + few, HDIM), BF16)] * 2,
    )
    dkv_wire, dq_wire, dk_own, dv_own = call(
        high_kernel, (shape(rows, 1280), shape(rows, 640), grad, grad),
        high_far, k_far, v_far, k_own, v_own, dk_far, dv_far, dq_low, dk_own, dv_own,
        scratch=[pltpu.VMEM((padded - few, HDIM), BF16)] * 2 + [pltpu.VMEM((padded, HDIM), F32)] * 2,
    )
    dkv_back = flipped(dkv_wire, 0, 1)
    dq_back = flipped(dq_wire, 0, 4)
    own_g = call(own_grads_kernel, shape(4, rows, 512, dtype=F32), dq_own, dk_own, dv_own)
    packed_g = call(pack_grads_kernel, shape(4, rows, 512), own_g, dkv_back, dq_back)
    held = [packed_g[0]] + to_chips(packed_g)
    other = flipped(jnp.stack([a[:, 256:] for a in held]), 1, 0)
    out = shape(rows, queries.shape[2])
    grads = call(
        unpack_grads_kernel, (out, out, out), *held, other,
        scratch=[pltpu.VMEM((4, rows, 256), BF16)] * 2,
    )
    return tuple(grad[None] for grad in grads)


def solution(mesh):
    placed = P(None, ("blk", "head"), None)
    on_grid = mesh.shape["head"] == 4 and mesh.shape["blk"] == 8
    return jax.shard_map(
        grid_body if on_grid else ring_body,
        mesh=mesh,
        in_specs=(placed,) * 5 + (P(None, "head", "blk"),),
        out_specs=(placed,) * 3,
        check_vma=False,
    )
```

```python
import functools
import math

import jax
import jax.numpy as jnp
from jax import lax
from jax.experimental import pallas as pl
from jax.experimental.pallas import tpu as pltpu
from jax.sharding import PartitionSpec as P

HDIM = 80
SCALING = HDIM ** (-0.5)
LOG2E = math.log2(math.e)
PADDED = 96
LOW = 3
LOW_KEYS = 3
VMEM_LIMIT = 24 * 1024 * 1024
F32 = jnp.float32
BF16 = jnp.bfloat16


def shifted(block, axis, distance):
    devices = range(lax.axis_size(axis))
    route = [((i - distance) % len(devices), i) for i in devices]
    return lax.ppermute(block, axis, route)


def tile_terms(query_h, cotan_h, lse_rows, delta_rows, key_h, value_h):
    query_rows = query_h.shape[0]
    key_rows = key_h.shape[0]
    groups = query_h.shape[1]
    scores = (
        jnp.einsum("qhd,khd->hqk", query_h, key_h, preferred_element_type=jnp.float32) * SCALING
    )
    probs = jnp.exp(scores - lse_rows[:, :, None])
    probs16 = probs.astype(jnp.bfloat16)
    value_part = jnp.einsum("hqk,qhd->khd", probs16, cotan_h, preferred_element_type=jnp.float32)
    dprobs = jnp.einsum("qhd,khd->hqk", cotan_h, value_h, preferred_element_type=jnp.float32)
    dscores = (probs * (dprobs - delta_rows[:, :, None])).astype(jnp.bfloat16)
    query_part = jnp.einsum("hqk,khd->qhd", dscores, key_h, preferred_element_type=jnp.float32)
    key_part = jnp.einsum("hqk,qhd->khd", dscores, query_h, preferred_element_type=jnp.float32)
    return (
        query_part.reshape(query_rows, groups * HDIM),
        key_part.reshape(key_rows, groups * HDIM),
        value_part.reshape(key_rows, groups * HDIM),
    )


def crop_terms(query_h, cotan_h, lse_rows, delta_rows, key_h, value_h):
    return lax.map(
        lambda pieces: tile_terms(*pieces), (query_h, cotan_h, lse_rows, delta_rows, key_h, value_h)
    )


def ring_body(queries, keys, values, outputs, grad_out, lse):
    crops = queries.shape[0]
    groups = lse.shape[1]
    rows = lse.shape[2]
    query_own, key_own, value_own, cotan_own, output_own = (
        lax.all_to_all(sent, "head", split_axis=2, concat_axis=1, tiled=True)
        for sent in (queries, keys, values, grad_out, outputs)
    )
    products = cotan_own.astype(jnp.float32) * output_own.astype(jnp.float32)
    delta_rows = jnp.transpose(
        jnp.sum(products.reshape(crops, rows, groups, HDIM), axis=-1), (0, 2, 1)
    )
    query_h = query_own.reshape(crops, rows, groups, HDIM)
    cotan_h = cotan_own.reshape(crops, rows, groups, HDIM)
    key_h = key_own.reshape(crops, rows, groups, HDIM)
    value_h = value_own.reshape(crops, rows, groups, HDIM)
    width = groups * HDIM
    nblocks = lax.axis_size("blk")
    zeros_acc = jnp.zeros((crops, rows, width), jnp.float32)
    start = (query_h, cotan_h, lse, delta_rows, zeros_acc, zeros_acc, zeros_acc)

    def cycle_step(index, carry):
        query_cur, cotan_cur, lse_cur, delta_cur, query_acc, key_acc, value_acc = carry
        query_part, key_part, value_part = crop_terms(
            query_cur, cotan_cur, lse_cur, delta_cur, key_h, value_h
        )
        query_acc, lse_cur, delta_cur = shifted(
            (query_acc + query_part, lse_cur, delta_cur), "blk", 1
        )
        query_cur, cotan_cur = shifted((query_cur, cotan_cur), "blk", 1)
        return (
            query_cur,
            cotan_cur,
            lse_cur,
            delta_cur,
            query_acc,
            key_acc + key_part,
            value_acc + value_part,
        )

    query_cur, cotan_cur, lse_cur, delta_cur, query_acc, key_acc, value_acc = lax.fori_loop(
        0, nblocks - 1, cycle_step, start
    )
    query_part, key_part, value_part = crop_terms(
        query_cur, cotan_cur, lse_cur, delta_cur, key_h, value_h
    )
    query_total = shifted((query_acc + query_part).astype(jnp.bfloat16), "blk", 1).astype(
        jnp.float32
    )
    grad_q16 = (query_total * SCALING).astype(jnp.bfloat16)
    grad_k16 = ((key_acc + key_part) * SCALING).astype(jnp.bfloat16)
    grad_v16 = (value_acc + value_part).astype(jnp.bfloat16)
    return tuple(
        lax.all_to_all(grad, "head", split_axis=1, concat_axis=2, tiled=True)
        for grad in (grad_q16, grad_k16, grad_v16)
    )


def call(kernel, out_shape, *operands, scratch=(), remote=0, out_space=pltpu.VMEM, limit=VMEM_LIMIT):
    specs = [
        pl.BlockSpec(memory_space=pltpu.HBM if i < remote else pltpu.VMEM)
        for i in range(len(operands))
    ]
    return pl.pallas_call(
        kernel,
        out_shape=out_shape,
        in_specs=specs,
        out_specs=jax.tree.map(lambda _: pl.BlockSpec(memory_space=out_space), out_shape),
        scratch_shapes=list(scratch),
        compiler_params=pltpu.CompilerParams(vmem_limit_bytes=limit),
    )(*operands)


def place():
    h, b = lax.axis_index("head"), lax.axis_index("blk")
    return lax.div(h, 2), lax.rem(lax.div(b, 2), 2), lax.rem(h, 2), h


def shape(*dims, dtype=BF16):
    return jax.ShapeDtypeStruct(dims, dtype)


def head_of(array, head):
    return array[:, HDIM * head : HDIM * (head + 1)]


def pieces_of(row):
    high = row.astype(BF16)
    rest = row - high.astype(F32)
    middle = rest.astype(BF16)
    low = (rest - middle.astype(F32)).astype(BF16)
    return jnp.concatenate([high.astype(F32), middle.astype(F32), low.astype(F32)], axis=0)


def pack_inputs_kernel(
    q_in, k_in, v_in, o_in, do_in, lse_in, out0, out1, out2, out3, give,
    q_s, k_s, v_s, o_s, do_s, lse_s, out_ref, done, sent,
):
    x, w, c, _ = place()
    copies = [
        pltpu.make_async_copy(source, target, done.at[i])
        for i, (source, target) in enumerate(
            ((q_in, q_s), (do_in, do_s), (k_in, k_s), (v_in, v_s), (o_in, o_s), (lse_in, lse_s))
        )
    ]
    for copy in copies:
        copy.start()
    for copy in copies[:4]:
        copy.wait()
    rows = q_s.shape[0]
    q, k, v, do = q_s[...], k_s[...], v_s[...], do_s[...]
    outs = (out0, out1, out2, out3)

    def leave(part, spot):
        mine = pltpu.make_async_copy(
            out_ref.at[0, spot, pl.ds(256, 384)], give.at[spot], sent.at[8 + part]
        )
        return [mine] + [
            pltpu.make_async_copy(out_ref.at[j, spot], out.at[spot], sent.at[4 * part + j])
            for j, out in enumerate(outs)
        ]

    for side in range(2):

        @pl.when(c == side)
        def _():
            for xs in range(2):
                for ws in range(2):
                    near, deep = [], []
                    for cs in (side, 1 - side):
                        head = 4 * xs + 2 * cs + ws
                        value = head_of(v, head)
                        near += [head_of(q, head), head_of(do, head), head_of(k, head), value[:, :16]]
                        deep.append(value[:, 16:])
                    j = 2 * (x ^ xs) + (w ^ ws)
                    out_ref[j, 0:rows] = jnp.concatenate(near + deep, axis=1)

    most = leave(0, pl.ds(0, PADDED - 16))
    for copy in most:
        copy.start()
    for copy in copies[4:]:
        copy.wait()
    products = do.astype(F32) * o_s[...].astype(F32)
    high = products.astype(BF16)
    rest = products - high.astype(F32)
    middle = rest.astype(BF16)
    low = (rest - middle.astype(F32)).astype(BF16)
    row = lax.broadcasted_iota(jnp.int32, (8, 640), 0)
    lane = lax.broadcasted_iota(jnp.int32, (8, 640), 1)
    mine = jnp.where((lane >= HDIM * row) & (lane < HDIM * (row + 1)), 1.0, 0.0).astype(BF16)
    deltas = sum(
        lax.dot_general(mine, part, (((1,), (1,)), ((), ())), preferred_element_type=F32)
        for part in (low, middle, high)
    )
    lse = lse_s[pl.ds(1 - w, 1), :] * LOG2E
    lse = jnp.concatenate([lse[:, rows * i : rows * (i + 1)] for i in range(4)], axis=0)
    lse = pieces_of(lse)
    blank = jnp.zeros((3, 128 - rows), F32)
    gap = jnp.zeros((5, 128), F32)
    edge = jnp.zeros((8, 128 - rows), F32)
    sides = [
        jnp.concatenate([lse[0:8], edge], axis=1),
        jnp.concatenate([jnp.concatenate([lse[8:12], lse[8:12]], axis=0), edge], axis=1),
    ]
    for xs in range(2):
        for ws in range(2):
            j = 2 * (x ^ xs) + (w ^ ws)
            pair = []
            for cs in range(2):
                head = 4 * xs + 2 * cs + ws
                delta = jnp.concatenate([pieces_of(deltas[head : head + 1, :]), blank], axis=1)
                pair.append(jnp.concatenate([delta, gap], axis=0))
            kept = jnp.where(c == 0, pair[0], pair[1])
            given = jnp.where(c == 0, pair[1], pair[0])
            spots = [kept, sides[0], given, sides[1], jnp.zeros((8, 128), F32)]
            out_ref[j, rows:PADDED] = jnp.concatenate(spots, axis=1).astype(BF16)
    last = leave(1, pl.ds(PADDED - 16, 16))
    for copy in last:
        copy.start()
    for copy in most + last:
        copy.wait()


def hold_kernel(block, held):
    held[...] = block[...]


def gather_queries_kernel(spots, *refs):
    *parts, near1, lse_in, wire, lse_s = refs
    rows = PADDED - 8
    _, w, _, h = place()
    own = lse_in[pl.ds(w, 1), :] * LOG2E
    below = near1[rows:PADDED, :].astype(F32)
    near = below[0:4, 128 : 128 + rows] + below[4:8, 128 : 128 + rows]
    near = near + below[0:4, 384 : 384 + rows]
    lse_s[...] = jnp.concatenate(
        [own[:, rows * i : rows * (i + 1)] for i in range(4)] + [near], axis=0
    )
    lower = []
    for (j, r), ref in zip(spots, parts):
        delta = ref[rows:PADDED, 0:128].astype(F32)[0:3, 0:rows]
        lse = lse_s[pl.ds(4 * (j % 2) + (h ^ (2 * (j // 2) + r)), 1), :]
        lower += [delta, pieces_of(lse)]
    lower = jnp.concatenate(lower + [jnp.zeros((32 - 6 * len(parts), rows), F32)], axis=0)
    wire[...] = jnp.concatenate(
        [ref[0:rows, 0:160] for ref in parts] + [lower.T.astype(BF16)], axis=1
    )


def gather_keys_kernel(spots, *refs):
    *parts, keys = refs
    rows = PADDED - 8
    pieces = []
    for (_, r), ref in zip(spots, parts):
        deep = 320 if r else 512
        pieces += [ref[0:rows, 160:256], ref[0:rows, deep : deep + 64]]
    keys[0:rows] = jnp.concatenate(pieces, axis=1)
    if keys.shape[0] > rows:
        keys[rows:PADDED] = jnp.zeros((PADDED - rows, keys.shape[1]), BF16)


def rows_of(wires):
    lse, delta = [], []
    for wire in wires:
        rows = wire.shape[0]
        count = wire.shape[1] // (2 * HDIM)
        gap = jnp.zeros((1, PADDED - rows), F32)
        pieces = wire[:, 2 * HDIM * count : 2 * HDIM * count + 32].astype(F32).T
        for i in range(0, 6 * count, 6):
            delta += [pieces[i : i + 1] + pieces[i + 1 : i + 2] + pieces[i + 2 : i + 3], gap]
            lse += [pieces[i + 3 : i + 4] + pieces[i + 4 : i + 5] + pieces[i + 5 : i + 6], gap]
    return jnp.concatenate(lse, axis=1), jnp.concatenate(delta, axis=1)


def spread(wide, left, right, first=0):
    rows = PADDED - 8
    blank = jnp.zeros((16, HDIM), BF16)
    for i in range(wide.shape[1] // (2 * HDIM)):
        at, lane = PADDED * (first + i), 2 * HDIM * i
        for target, start in ((left, lane), (right, lane + HDIM)):
            target[pl.ds(at + PADDED - 16, 16), :] = blank
            target[pl.ds(at, rows), :] = wide[0:rows, start : start + HDIM]


def tile_step(q, do, k_s, v_s, lse, delta, chunk=768):
    q_t, do_t = q.T, do.T
    k_t = k_s[...].T
    dq_t = None
    parts = []
    for start in range(0, k_s.shape[0], chunk):
        spot = slice(start, start + chunk)
        k, v = k_s[spot, :], v_s[spot, :]
        scores = jnp.dot(k, q_t, preferred_element_type=F32)
        probs = jnp.exp2(scores * (SCALING * LOG2E) - lse)
        dv = jnp.dot(probs.astype(BF16), do, preferred_element_type=F32)
        dprobs = jnp.dot(v, do_t, preferred_element_type=F32)
        dscores = (probs * (dprobs - delta)).astype(BF16)
        dk = jnp.dot(dscores, q, preferred_element_type=F32)
        more = jnp.dot(k_t[:, spot], dscores, preferred_element_type=F32)
        dq_t = more if dq_t is None else dq_t + more
        parts.append((spot, dk, dv))
    return dq_t, parts


def to_wire(arrays, rows):
    count = arrays[0].shape[0] // PADDED
    return jnp.concatenate(
        [a[PADDED * i : PADDED * i + rows].astype(BF16) for i in range(count) for a in arrays],
        axis=1,
    )


def own_own_kernel(low, high, k_low, k_high, dq_t, dk, dv, q_s, do_s, k_s, v_s):
    spread(low, q_s, do_s)
    spread(high, q_s, do_s, LOW)
    spread(k_low, k_s, v_s)
    spread(k_high, k_s, v_s, LOW_KEYS)
    dq_t[...], parts = tile_step(q_s[...], do_s[...], k_s, v_s, *rows_of([low, high]))
    for spot, dk_part, dv_part in parts:
        dk[spot, :] = dk_part
        dv[spot, :] = dv_part


def low_own_kernel(wire, k_own, v_own, dk_in, dv_in, dq_t, dk, dv, q_s, do_s):
    spread(wire, q_s, do_s)
    dq_t[...], parts = tile_step(q_s[...], do_s[...], k_own, v_own, *rows_of([wire]))
    for spot, dk_part, dv_part in parts:
        dk[spot, :] = dk_in[spot, :] + dk_part
        dv[spot, :] = dv_in[spot, :] + dv_part


def far_keys_kernel(
    low, high, low_far, q_s, do_s, q_low_s, do_low_s, k_low, k_high, dq_before, dq_low_before,
    dq_t, dq_low, dk, dv, k_s, v_s, all_q, all_do,
):
    spread(k_low, k_s, v_s)
    spread(k_high, k_s, v_s, LOW_KEYS)
    own = q_s.shape[0]
    all_q[0:own], all_q[own:] = q_s[...], q_low_s[...]
    all_do[0:own], all_do[own:] = do_s[...], do_low_s[...]
    more, parts = tile_step(
        all_q[...], all_do[...], k_s, v_s, *rows_of([low, high, low_far])
    )
    dq_t[...] = dq_before[...] + more[:, 0:own]
    dq_low[...] = dq_low_before[...] + more[:, own:]
    for spot, dk_part, dv_part in parts:
        dk[spot, :] = dk_part
        dv[spot, :] = dv_part


def high_kernel(
    wire, k_far, v_far, k_own, v_own, dk_far, dv_far, dq_low, dk_in, dv_in,
    dkv_wire, dq_wire, dk_own, dv_own, q_s, do_s, dk, dv,
):
    spread(wire, q_s, do_s)
    q, do = q_s[...], do_s[...]
    rows = rows_of([wire])
    first, parts = tile_step(q, do, k_far, v_far, *rows)
    for spot, dk_part, dv_part in parts:
        dk[spot, :] = (dk_far[spot, :] + dk_part) * SCALING
        dv[spot, :] = dv_far[spot, :] + dv_part
    dkv_wire[...] = to_wire([dk[...], dv[...]], dkv_wire.shape[0])
    more, parts = tile_step(q, do, k_own, v_own, *rows)
    dq = jnp.concatenate([dq_low[...], first + more], axis=1) * SCALING
    dq_wire[...] = to_wire([dq.T], dq_wire.shape[0])
    for spot, dk_part, dv_part in parts:
        dk_own[spot, :] = dk_in[spot, :] + dk_part
        dv_own[spot, :] = dv_in[spot, :] + dv_part


def own_grads_kernel(dq_t, dk, dv, out):
    rows = out.shape[1]
    dq = dq_t[...].T * SCALING
    zeros = jnp.zeros((rows, 16), F32)
    for i in range(8):
        spot = slice(PADDED * i, PADDED * i + rows)
        block = jnp.concatenate([dq[spot], dk[spot, :] * SCALING, dv[spot, :], zeros], axis=1)
        out[i // 2, :, 256 * (i % 2) : 256 * (i % 2) + 256] = block


def pack_grads_kernel(own, dkv_wire, dq_wire, out):
    rows = dkv_wire.shape[0]
    dq = dq_wire[...]
    dkv = dkv_wire[...]
    zeros = jnp.zeros((rows, 16), BF16)
    for i in range(8):
        block = jnp.concatenate(
            [
                dq[:, HDIM * i : HDIM * (i + 1)],
                dkv[:, 2 * HDIM * i : 2 * HDIM * (i + 1)],
                zeros,
            ],
            axis=1,
        )
        lanes = slice(256 * (i % 2), 256 * (i % 2) + 256)
        out[i // 2, :, lanes] = (own[i // 2, :, lanes] + block.astype(F32)).astype(BF16)


def unpack_grads_kernel(*refs):
    kept, given, dq, dk, dv, held, other = refs[0:4], refs[4], *refs[5:]
    x, w, c, _ = place()
    for j in range(4):
        held[j] = kept[j][:, 0:256]
        other[j] = given[j]
    blocks = []
    for head in range(8):
        xs, cs, ws = head // 4, (head // 2) % 2, head % 2
        j = 2 * (x ^ xs) + (w ^ ws)
        blocks.append(jnp.where(c == cs, held[j].astype(F32), other[j].astype(F32)).astype(BF16))
    for k, out in enumerate((dq, dk, dv)):
        out[...] = jnp.concatenate(
            [block[:, HDIM * k : HDIM * (k + 1)] for block in blocks], axis=1
        )


def flipped(array, head_bits, blk_bits):
    heads, blks = lax.axis_size("head"), lax.axis_size("blk")
    if not blk_bits:
        return lax.ppermute(array, "head", [(i, i ^ head_bits) for i in range(heads)])
    if not head_bits:
        return lax.ppermute(array, "blk", [(i, i ^ blk_bits) for i in range(blks)])
    bits = head_bits * blks + blk_bits
    return lax.ppermute(array, ("head", "blk"), [(i, i ^ bits) for i in range(heads * blks)])


def to_chips(packed):
    return [flipped(packed[1], 0, 2), flipped(packed[2], 2, 0), flipped(packed[3], 2, 2)]


def grid_body(queries, keys, values, outputs, grad_out, lse):
    rows = queries.shape[1]
    padded = 8 * PADDED
    few = LOW * PADDED

    packed = call(
        pack_inputs_kernel,
        (shape(PADDED, 640),) * 4 + (shape(PADDED, 384),),
        queries[0], keys[0], values[0], outputs[0], grad_out[0], lse[0],
        remote=6,
        out_space=pltpu.HBM,
        limit=57 * 1024 * 1024,
        scratch=[pltpu.VMEM(queries.shape[1:], BF16)] * 5
        + [pltpu.VMEM(lse.shape[1:], F32), pltpu.VMEM((4, PADDED, 640), BF16)]
        + [pltpu.SemaphoreType.DMA((6,)), pltpu.SemaphoreType.DMA((10,))],
    )
    own = call(hold_kernel, shape(PADDED, 640), packed[0])
    near = to_chips(packed)
    other = [flipped(a, 1, 0) for a in [packed[4]] + [b[:, 256:] for b in near]]
    blocks = [ref for pair in zip([own] + near, other) for ref in pair]
    spots = [(j, r) for j in range(4) for r in range(2)]

    def gather_queries(first, last):
        return call(
            functools.partial(gather_queries_kernel, spots[first:last]),
            shape(rows, 160 * (last - first) + 32),
            *blocks[first:last], near[0], lse[0],
            scratch=[pltpu.VMEM((8, rows), F32)],
        )

    def gather_keys(first, last, tall):
        return call(
            functools.partial(gather_keys_kernel, spots[first:last]),
            shape(tall, 160 * (last - first)),
            *blocks[first:last],
        )

    low, k_low = gather_queries(0, LOW), gather_keys(0, LOW_KEYS, PADDED)
    low_far, k_low_far = flipped(low, 0, 4), flipped(k_low, 0, 1)
    high, k_high = gather_queries(LOW, 8), gather_keys(LOW_KEYS, 8, rows)
    high_far = flipped(high, 0, 4)
    k_high, k_low_far, low_far = lax.optimization_barrier((k_high, k_low_far, low_far))
    k_high_far = flipped(k_high, 0, 1)
    keys_far = [k_low_far, k_high_far]

    grad = shape(padded, HDIM, dtype=F32)
    side = shape(padded, HDIM)
    dq_shape = shape(HDIM, padded, dtype=F32)
    dq_own, dk_own, dv_own, q_s, do_s, k_own, v_own = call(
        own_own_kernel, (dq_shape, grad, grad, side, side, side, side), low, high, k_low, k_high
    )
    some = shape(few, HDIM)
    dq_low, dk_own, dv_own, q_low_s, do_low_s = call(
        low_own_kernel, (shape(HDIM, few, dtype=F32), grad, grad, some, some),
        low_far, k_own, v_own, dk_own, dv_own,
    )
    dq_own, dq_low, dk_far, dv_far, k_far, v_far = call(
        far_keys_kernel, (dq_shape, shape(HDIM, few, dtype=F32), grad, grad, side, side),
        low, high, low_far, q_s, do_s, q_low_s, do_low_s, *keys_far, dq_own, dq_low,
        scratch=[pltpu.VMEM((padded + few, HDIM), BF16)] * 2,
    )
    dkv_wire, dq_wire, dk_own, dv_own = call(
        high_kernel, (shape(rows, 1280), shape(rows, 640), grad, grad),
        high_far, k_far, v_far, k_own, v_own, dk_far, dv_far, dq_low, dk_own, dv_own,
        scratch=[pltpu.VMEM((padded - few, HDIM), BF16)] * 2 + [pltpu.VMEM((padded, HDIM), F32)] * 2,
    )
    dkv_back = flipped(dkv_wire, 0, 1)
    dq_back = flipped(dq_wire, 0, 4)
    own_g = call(own_grads_kernel, shape(4, rows, 512, dtype=F32), dq_own, dk_own, dv_own)
    packed_g = call(pack_grads_kernel, shape(4, rows, 512), own_g, dkv_back, dq_back)
    held = [packed_g[0]] + to_chips(packed_g)
    other = flipped(jnp.stack([a[:, 256:] for a in held]), 1, 0)
    out = shape(rows, queries.shape[2])
    grads = call(
        unpack_grads_kernel, (out, out, out), *held, other,
        scratch=[pltpu.VMEM((4, rows, 256), BF16)] * 2,
    )
    return tuple(grad[None] for grad in grads)


def solution(mesh):
    placed = P(None, ("blk", "head"), None)
    on_grid = mesh.shape["head"] == 4 and mesh.shape["blk"] == 8
    return jax.shard_map(
        grid_body if on_grid else ring_body,
        mesh=mesh,
        in_specs=(placed,) * 5 + (P(None, "head", "blk"),),
        out_specs=(placed,) * 3,
        check_vma=False,
    )
```
